256 devices in a mesh: dp: 32 (over y, z_lo, core), tensor: 8 (over z_hi, x).
Axes of the slice: x: 4, y: 4, z: 8 (z_hi: 2, z_lo: 4; z = z_hi * 4 + z_lo), core: 2. Of those that a mesh axis runs over, the one named last changes fastest.
Arguments:
- tokens: bfloat16 [8192, 4096], P('dp'), may hold values from -6 to 6
- gate_values: bfloat16 [8192, 14336], P('dp', 'tensor'), may hold values from -6 to 6
- up_latent: float32 [4096, 14336], P('dp', 'tensor'), may hold values from -6.25 to 6.25
- hidden_grad: bfloat16 [8192, 14336], P('dp', 'tensor'), may hold values from -100 to 100
Outputs:
- hidden: bfloat16 [8192, 14336], P('dp', 'tensor')
- gate_grad: bfloat16 [8192, 14336], P('dp', 'tensor')
- token_grad: bfloat16 [8192, 4096], P('dp', 'tensor')
- up_grad: float32 [4096, 14336], P('dp', 'tensor')
The draws below stay inside these ranges and needn't reach their ends.
All inputs are finite; a program needn't handle non-finite values.
Results may differ from the reference program's by a relative error of at most 0.03.
Values may be sent and summed in bfloat16 or wider, within the bound.
A program may use at most 128 MiB of HBM per device.

```python
import math
import jax
import jax.numpy as jnp
from jax import lax

D = 4096
FF = 14336
TOK_DEV = 256
TOKENS = 8192
N_DP = 32
N_TENSOR = 8


def draw_up_latent(key, part):
    key = jax.random.fold_in(key, 11)
    key_base, key_rows, key_cols, key_side = jax.random.split(key, 4)
    base = jnp.clip(jax.random.normal(key_base, (D, FF), jnp.float32), -6.0, 6.0)
    rise = 3.0
    row_place = jnp.arange(D, dtype=jnp.float32) / max(D - 1, 1)
    col_place = jnp.arange(FF, dtype=jnp.float32) / max(FF - 1, 1)
    row_factor = jnp.exp(jax.random.uniform(key_rows, (D,), jnp.float32) * math.log(10.0)) * rise ** row_place / 6.0
    col_factor = jnp.exp(jax.random.uniform(key_cols, (FF,), jnp.float32) * math.log(10.0)) * rise ** col_place / 6.0
    latent = base * row_factor[:, None] * col_factor[None, :] / math.sqrt(D)
    magnitude = jnp.abs(latent)
    mean_size = jnp.mean(magnitude)
    inside = (magnitude > 0.35 * mean_size) & (magnitude < 0.65 * mean_size)
    upper_side = jax.random.bernoulli(key_side, 0.5, (D, FF))
    moved = jnp.where(upper_side, 0.75 * mean_size, 0.25 * mean_size)
    signs = jnp.where(latent < 0.0, jnp.float32(-1.0), jnp.float32(1.0))
    return jnp.where(inside, signs * moved, latent)


def draw_hidden_grad(key, part):
    key = jax.random.fold_in(key, 23)
    key_base, key_rows, key_cols = jax.random.split(key, 3)
    base = jnp.clip(jax.random.normal(key_base, (TOKENS, FF), jnp.float32), -4.0, 4.0)
    rise = 3.0
    row_place = jnp.arange(TOKENS, dtype=jnp.float32) / max(TOKENS - 1, 1)
    row_factor = jnp.exp(jax.random.uniform(key_rows, (TOKENS,), jnp.float32) * math.log(10.0)) * rise ** row_place / 5.0
    col_factor = jnp.exp(jax.random.uniform(key_cols, (FF,), jnp.float32) * math.log(10.0)) / 5.0
    return (base * row_factor[:, None] * col_factor[None, :]).astype(jnp.bfloat16)


def levels(stream_key, extent, shards, low, largest):
    loudness = 1.0
    for dim, shards_of in shards:
        steps = jax.random.uniform(jax.random.fold_in(jax.random.fold_in(stream_key, 6), dim), (shards_of,), jnp.float32, low / len(shards), largest / len(shards))
        loudness = loudness * jnp.repeat(jnp.exp(steps), extent[dim] // shards_of).reshape((-1,) + (1,) * (len(extent) - 1 - dim))
    return loudness


def gaussian(key, shape, scale, bound, shards=(), kind=jnp.bfloat16):
    factor_of = levels(key, shape, shards, -0.22, 0.18) if shards else 1.0
    array = jax.random.normal(key, shape, jnp.float32) * scale * factor_of
    return jnp.minimum(jnp.maximum(array, -bound), bound).astype(kind)


def setup_inputs(seed: int = 0) -> dict:
    key_of = jax.random.split(jax.random.key(seed), 5)
    tokens = gaussian(key_of[0], (TOKENS, D), 1.0, 6.0, ((0, 32),))
    gate_values = gaussian(key_of[1], (TOKENS, FF), 1.5, 6.0, ((0, 32), (1, 8)))
    up_latent = draw_up_latent(jax.random.fold_in(key_of[4], 71), 0)
    hidden_grad = draw_hidden_grad(jax.random.fold_in(key_of[4], 71), 0)
    return dict(tokens=tokens, gate_values=gate_values, up_latent=up_latent, hidden_grad=hidden_grad)


EPSILON = 1e-5


def ternarize(latent_wide, scale_value):
    keep = jnp.abs(latent_wide) > 0.5 * scale_value
    signs = jnp.where(keep, jnp.sign(latent_wide), jnp.float32(0.0))
    return (signs * scale_value).astype(jnp.bfloat16)


def reference(tokens, gate_values, up_latent, hidden_grad):
    latent_half = up_latent.astype(jnp.bfloat16)
    latent_wide = lax.optimization_barrier(latent_half).astype(jnp.float32)
    scale_value = jnp.sum(jnp.abs(latent_wide)) / (D * FF) + EPSILON
    weight = ternarize(latent_wide, scale_value)
    up_value = jnp.dot(tokens, weight, preferred_element_type=jnp.float32)
    gate_wide = gate_values.astype(jnp.float32)
    sigmoid_gate = jax.nn.sigmoid(gate_wide)
    activated = gate_wide * sigmoid_gate
    hidden = (activated * up_value).astype(jnp.bfloat16)
    cotangent = hidden_grad.astype(jnp.float32)
    up_cot = (cotangent * activated).astype(jnp.bfloat16)
    gate_grad = (cotangent * up_value * sigmoid_gate * (1.0 + gate_wide * (1.0 - sigmoid_gate))).astype(jnp.bfloat16)
    block_width = FF // N_TENSOR
    token_total = jnp.zeros((TOKENS, D), jnp.float32)
    for block in range(N_TENSOR):
        lower = block * block_width
        upper = lower + block_width
        term = lax.dot_general(up_cot[:, lower:upper], weight[:, lower:upper], (((1,), (1,)), ((), ())), preferred_element_type=jnp.float32)
        token_total = token_total + lax.optimization_barrier(term.astype(jnp.bfloat16)).astype(jnp.float32)
    token_grad = token_total.astype(jnp.bfloat16)

    def add_block(index, total):
        start = (index * TOK_DEV).astype(jnp.int32)
        token_block = lax.dynamic_slice_in_dim(tokens, start, TOK_DEV, 0)
        cot_block = lax.dynamic_slice_in_dim(up_cot, start, TOK_DEV, 0)
        term = lax.dot_general(token_block, cot_block, (((0,), (0,)), ((), ())), preferred_element_type=jnp.float32)
        return total + lax.optimization_barrier(term.astype(jnp.bfloat16)).astype(jnp.float32)

    up_grad = lax.fori_loop(jnp.int32(0), jnp.int32(N_DP), add_block, jnp.zeros((D, FF), jnp.float32))
    return hidden, gate_grad, token_grad, up_grad
```

```python
import functools

import jax
import jax.numpy as jnp
from jax import lax
from jax.experimental import pallas as pl
from jax.experimental.pallas import tpu as pltpu
from jax.sharding import PartitionSpec as P

D = 4096
FF = 14336
TOK = 256
COLS = 1792
HALF = COLS // 2
ROWS = 128
BLOCK = 1024
EPSILON = 1e-05
MESH = pl.DeviceIdType.MESH
F32 = jnp.float32
BF16 = jnp.bfloat16


def kernel(
    tokens, gate, latent, cot,
    hidden_out, gate_out, token_out, up_out,
    lat32, wg, wt, tokg, tokt, ucg, gate_v, cot_v,
    gp, gxs, gxr, gsend, grl, grr,
    pvf, pvs, fwd, chain, direct,
    tt_own, tt_send, tt_recv, zsend, zrecv, fsend, tgr,
    s1, s2, s3,
    in_sem, zr_sem, zsr_sem, zsl_sem, cs_sem, cr_sem,
    yrs, yrr, yls, ylr, tks, tkr,
    s1s, s1r, s2s, s2r, s3s, s3r,
    gcs, gcr, gls, glr, grs, grr_sem,
    ops, opr, tts, ttr, zxs, zxr, fs, fr,
):
    me_dp = lax.axis_index("dp")
    me_t = lax.axis_index("tensor")
    y = me_dp // 8
    g8 = me_dp % 8
    zl = g8 // 2
    k = g8 % 2
    x = me_t % 4
    zh = me_t // 4

    def dp_of(yy, zz, kk):
        return yy * 8 + zz * 2 + kk

    def at_y(d):
        return (((y + d) % 4) * 8 + g8, me_t)

    def at_z(zz):
        return (dp_of(y, zz, k), me_t)

    other = (dp_of(y, zl, 1 - k), me_t)

    def at_x(d):
        return (me_dp, zh * 4 + (x + d) % 4)

    flip = (me_dp, (1 - zh) * 4 + x)

    def rcopy(src, dst, ssem, rsem, dev):
        return pltpu.make_async_remote_copy(
            src_ref=src, dst_ref=dst, send_sem=ssem, recv_sem=rsem,
            device_id=dev, device_id_type=MESH,
        )

    source_x, source_y = y, 2 * zh + x // 2
    self_source = jnp.logical_and(source_x == x, source_y == y)
    collects = zh == y // 2

    def final_dev(j):
        return (dp_of(x, zl, k), zh * 4 + 2 * (y % 2) + j)

    def final_self(j):
        return jnp.logical_and(x == y, 2 * (y % 2) + j == x)

    lat_in = pltpu.make_async_copy(latent, lat32, in_sem.at[0])
    gate_in = pltpu.make_async_copy(gate, gate_v, in_sem.at[1])
    cot_in = pltpu.make_async_copy(cot, cot_v, in_sem.at[2])
    tok_in = pltpu.make_async_copy(
        tokens.at[:, pl.ds(pl.multiple_of(y * BLOCK, BLOCK), BLOCK)],
        tokg.at[pl.ds(pl.multiple_of(y * TOK, TOK), TOK)],
        in_sem.at[3],
    )
    lat_in.start()
    gate_in.start()
    cot_in.start()
    tok_in.start()

    barrier = pltpu.get_barrier_semaphore()

    def greet(dev):
        pl.semaphore_signal(barrier, inc=1, device_id=dev, device_id_type=MESH)

    for d in range(1, 4):
        greet(at_y(d))
    for d in range(1, 8):
        greet((y * 8 + (g8 + d) % 8, me_t))
        greet((me_dp, (me_t + d) % 8))

    @pl.when(jnp.logical_not(self_source))
    def _():
        greet((dp_of(source_y, zl, k), zh * 4 + source_x))

    takers = jnp.int32(2)
    for j in range(2):
        takers = takers - jnp.where(final_self(j), 1, 0)
    pl.semaphore_wait(barrier, 17 + jnp.where(collects, takers, 0))

    def tok_send(d):
        yy = (y + d) % 4
        return rcopy(
            tokens.at[:, pl.ds(pl.multiple_of(yy * BLOCK, BLOCK), BLOCK)],
            tokg.at[pl.ds(pl.multiple_of(y * TOK, TOK), TOK)],
            tks.at[d], tkr.at[d], at_y(d),
        )

    for d in (1, 3, 2):
        tok_send(d).start()

    lat_in.wait()
    part = jnp.zeros((8, 128), F32)

    def cast_rows(i, acc):
        rows = pl.ds(pl.multiple_of(i * 16, 16), 16)
        half = lat32[rows, :].astype(BF16)
        wg[zl, k, rows, :] = half
        mag = jnp.abs(half.astype(F32))
        mag = mag[0:8] + mag[8:16]
        tot = mag[:, 0:128]
        for c in range(1, COLS // 128):
            tot = tot + mag[:, c * 128:(c + 1) * 128]
        return acc + tot

    part = lax.fori_loop(0, ROWS // 16, cast_rows, part)

    def z_right(b):
        return rcopy(wg.at[b, k], wg.at[b, k], zsr_sem.at[b], zr_sem.at[b], at_z(lax.rem(zl + 1, 4)))

    def z_left(b):
        return rcopy(wg.at[b, k], wg.at[b, k], zsl_sem.at[b], zr_sem.at[b], at_z(lax.rem(zl + 3, 4)))

    def c_send(b):
        return rcopy(wg.at[b, k], wg.at[b, k], cs_sem.at[b], cr_sem.at[b], other)

    def c_recv(b):
        return rcopy(wg.at[b, k], wg.at[b, 1 - k], cs_sem.at[b], cr_sem.at[b], other)

    @pl.when(zl < 3)
    def _():
        z_right(zl).start()

    @pl.when(zl > 0)
    def _():
        z_left(zl).start()

    c_send(zl).start()

    s1[g8] = part

    def s1_copy(d):
        return rcopy(s1.at[g8], s1.at[g8], s1s.at[d], s1r.at[d], (y * 8 + (g8 + d) % 8, me_t))

    def s2_copy(d):
        return rcopy(s2.at[y], s2.at[y], s2s.at[d], s2r.at[d], at_y(d))

    def s3_copy(d):
        return rcopy(s3.at[me_t], s3.at[me_t], s3s.at[d], s3r.at[d], (me_dp, (me_t + d) % 8))

    for d in range(1, 8):
        s1_copy(d).start()

    gate_in.wait()
    cot_in.wait()

    def cot_rows(lo, hi):
        @pl.loop(lo // 16, hi // 16)
        def _(i):
            rows = pl.ds(pl.multiple_of(i * 16, 16), 16)
            g = gate_v[rows, :].astype(F32)
            act = g * jax.nn.sigmoid(g)
            to = pl.ds(pl.multiple_of(y * TOK + i * 16, 16), 16)
            ucg[to, :] = (cot_v[rows, :].astype(F32) * act).astype(BF16)

    def uc_half(yy, h):
        return ucg.at[pl.ds(pl.multiple_of((yy % 4) * TOK + h * 128, 128), 128)]

    def y_right(i):
        piece = (uc_half(y, 0), uc_half(y, 1), uc_half(y + 3, 0))[i]
        return rcopy(piece, piece, yrs.at[i], yrr.at[i], at_y(1))

    def y_left(i):
        piece = (uc_half(y, 1), uc_half(y, 0), uc_half(y + 1, 1))[i]
        return rcopy(piece, piece, yls.at[i], ylr.at[i], at_y(3))

    cot_rows(0, 128)
    y_right(0).start()
    cot_rows(128, 256)
    y_left(0).start()
    y_right(1).start()
    y_left(1).start()

    for d in range(1, 8):
        s1_copy(d).wait_recv()
    tot = s1[0]
    for i in range(1, 8):
        tot = tot + s1[i]
    s2[y] = tot
    for d in range(1, 4):
        s2_copy(d).start()
    for d in range(1, 4):
        s2_copy(d).wait_recv()
    tot = s2[0]
    for i in range(1, 4):
        tot = tot + s2[i]
    s3[me_t] = tot
    for d in range(1, 8):
        s3_copy(d).start()
    for d in range(1, 8):
        s3_copy(d).wait_recv()
    tot = s3[0]
    for i in range(1, 8):
        tot = tot + s3[i]
    total = jnp.sum(jnp.sum(tot, axis=0, keepdims=True), axis=1, keepdims=True)
    scale = total / (D * FF) + EPSILON

    def z_step(s):
        left, right = zl - s, zl + s

        @pl.when(left >= 0)
        def _():
            b = lax.rem(left + 4, 4)
            z_right(b).wait_recv()

            @pl.when(zl < 3)
            def _():
                z_right(b).start()

            c_send(b).start()

        @pl.when(right <= 3)
        def _():
            b = lax.rem(right, 4)
            z_left(b).wait_recv()

            @pl.when(zl > 0)
            def _():
                z_left(b).start()

            c_send(b).start()

    z_step(1)
    y_right(0).wait_recv()
    y_right(2).start()
    y_left(0).wait_recv()
    y_left(2).start()
    z_step(2)
    y_right(1).wait_recv()
    y_left(1).wait_recv()
    tok_in.wait()
    for d in (1, 3, 2):
        tok_send(d).wait_recv()
    z_step(3)
    for b in range(4):
        c_recv(b).wait_recv()

    bound = 0.5 * scale
    plus = scale.astype(BF16).astype(F32)

    @pl.loop(0, BLOCK // 16)
    def _(i):
        b, r = i // 16, i % 16
        wide = wg[b, r // 8, pl.ds(pl.multiple_of((r % 8) * 16, 16), 16), :].astype(F32)
        tern = jnp.where(wide > bound, plus, jnp.where(wide < -bound, -plus, 0.0))
        wt[pl.ds(pl.multiple_of(i * 16, 16), 16), :] = tern.astype(BF16)

    y_right(2).wait_recv()
    y_left(2).wait_recv()

    def m1(target):
        cols = pl.ds(pl.multiple_of(target * 256, 256), 256)
        tokt[...] = tokg[:, cols].T

        @pl.loop(0, 7)
        def _(n):
            at = pl.ds(pl.multiple_of(n * 256, 256), 256)
            gp[target, :, at] = jnp.dot(tokt[...], ucg[:, at], preferred_element_type=F32)

        theirs = pl.ds(pl.multiple_of((1 - k) * ROWS, ROWS), ROWS)
        gxs[target] = gp[target, theirs, :].astype(BF16)
        g_cross(target).start()

    def g_cross(target):
        return rcopy(gxs.at[target], gxr.at[target], gcs.at[target], gcr.at[target], other)

    def g_right(target):
        return rcopy(gsend.at[target], grl.at[target], grs.at[target], glr.at[target], at_z(lax.rem(zl + 1, 4)))

    def g_left(target):
        return rcopy(gsend.at[target], grr.at[target], gls.at[target], grr_sem.at[target], at_z(lax.rem(zl + 3, 4)))

    mine = pl.ds(pl.multiple_of(k * ROWS, ROWS), ROWS)

    def combine(target):
        g_cross(target).wait_recv()

        @pl.when(target > zl)
        def _():
            @pl.when(zl == 0)
            def _():
                gsend[target] = (gp[target, mine, :] + gxr[target].astype(F32)).astype(BF16)

            @pl.when(zl > 0)
            def _():
                g_right(target).wait_recv()
                gsend[target] = (
                    gp[target, mine, :] + gxr[target].astype(F32) + grl[target].astype(F32)
                ).astype(BF16)

            g_right(target).start()

        @pl.when(target < zl)
        def _():
            @pl.when(zl == 3)
            def _():
                gsend[target] = (gp[target, mine, :] + gxr[target].astype(F32)).astype(BF16)

            @pl.when(zl < 3)
            def _():
                g_left(target).wait_recv()
                gsend[target] = (
                    gp[target, mine, :] + gxr[target].astype(F32) + grr[target].astype(F32)
                ).astype(BF16)

            g_left(target).start()

    def pick(a0, a1, a2, a3):
        return jnp.where(zl == 0, a0, jnp.where(zl == 1, a1, jnp.where(zl == 2, a2, a3)))

    order = [pick(3, 3, 0, 0), pick(2, 0, 3, 1), pick(1, 2, 1, 2), zl]
    edge = jnp.logical_or(zl == 0, zl == 3)

    def m2(slot, yy):
        rows = pl.ds(pl.multiple_of((yy % 4) * TOK, TOK), TOK)

        @pl.loop(0, 7)
        def _(n):
            at = pl.ds(pl.multiple_of(n * 256, 256), 256)
            pvf[slot, :, at] = jnp.dot(tokg[rows, :], wt[:, at], preferred_element_type=F32)

    A, B = pl.ds(0, HALF), pl.ds(HALF, HALF)

    def p_minus(i):
        slot, cols = ((0, A), (1, B), (1, A))[i]
        dst = (fwd, direct, chain)[i]
        return rcopy(pvs.at[slot, :, cols], dst.at[:, cols], ops.at[0, i], opr.at[0, i], at_y(3))

    def p_plus(i):
        slot, cols = ((0, B), (2, A), (2, B))[i]
        dst = (fwd, direct, chain)[i]
        return rcopy(pvs.at[slot, :, cols], dst.at[:, cols], ops.at[1, i], opr.at[1, i], at_y(1))

    m1(order[0])
    m2(0, y + 2)
    pvs[0] = pvf[0].astype(BF16)
    p_minus(0).start()
    p_plus(0).start()

    @pl.when(edge)
    def _():
        combine(order[0])

    m2(1, y + 3)
    pvs[1, :, B] = pvf[1, :, B].astype(BF16)
    p_minus(1).start()
    m2(2, y + 1)
    pvs[2, :, A] = pvf[2, :, A].astype(BF16)
    p_plus(1).start()

    def m3(xx):
        rows = pl.ds(pl.multiple_of(xx * TOK, TOK), TOK)

        @pl.loop(0, 4)
        def _(n):
            at = pl.ds(pl.multiple_of(n * 256, 256), 256)
            tt_own[:, at] = lax.dot_general(
                ucg[rows, :], wt[at, :], (((1,), (1,)), ((), ())), preferred_element_type=F32
            )

    def t_send(d):
        return rcopy(tt_send.at[d - 1], tt_recv.at[d - 1], tts.at[d], ttr.at[d], at_x(d))

    for d in (2, 1, 3):
        m3((x + d) % 4)
        tt_send[d - 1] = tt_own[...].astype(BF16)
        t_send(d).start()
    m3(x)

    m1(order[1])

    @pl.when(edge)
    def _():
        combine(order[1])

    m1(order[2])

    @pl.when(edge)
    def _():
        combine(order[2])

    m1(order[3])

    @pl.when(jnp.logical_not(edge))
    def _():
        combine(order[0])

    p_minus(0).wait_recv()
    pvs[1, :, A] = (pvf[1, :, A] + fwd[:, A].astype(F32)).astype(BF16)
    p_minus(2).start()
    p_plus(0).wait_recv()
    pvs[2, :, B] = (pvf[2, :, B] + fwd[:, B].astype(F32)).astype(BF16)
    p_plus(2).start()

    m2(0, y)

    @pl.when(jnp.logical_not(edge))
    def _():
        combine(order[1])
        combine(order[2])

    for d in range(1, 4):
        t_send(d).wait_recv()

    @pl.loop(0, TOK // 16)
    def _(i):
        rows = pl.ds(pl.multiple_of(i * 16, 16), 16)
        total = tt_own[rows, :]
        for d in range(3):
            total = total + tt_recv[d, rows, :].astype(F32)
        tt_own[rows, :] = total
        zsend[rows, :] = total.astype(BF16)

    z_copy = rcopy(zsend, zrecv, zxs, zxr, flip)

    @pl.when(jnp.logical_not(collects))
    def _():
        z_copy.start()

    def f_send(j):
        return rcopy(fsend.at[j], tgr, fs.at[j], fr, final_dev(j))

    @pl.when(collects)
    def _():
        z_copy.wait_recv()
        for j in range(2):
            cols = pl.ds(j * 512, 512)
            fsend[j] = (tt_own[:, cols] + zrecv[:, cols].astype(F32)).astype(BF16)

            @pl.when(jnp.logical_not(final_self(j)))
            def _():
                f_send(j).start()

            @pl.when(final_self(j))
            def _():
                tgr[...] = fsend[j]

    p_minus(1).wait_recv()
    p_plus(1).wait_recv()
    p_minus(2).wait_recv()
    p_plus(2).wait_recv()

    @pl.loop(0, TOK // 16)
    def _(i):
        rows = pl.ds(pl.multiple_of(i * 16, 16), 16)
        up = pvf[0, rows, :] + chain[rows, :].astype(F32) + direct[rows, :].astype(F32)
        g = gate_v[rows, :].astype(F32)
        sig = jax.nn.sigmoid(g)
        hidden_out[rows, :] = (g * sig * up).astype(BF16)
        gate_out[rows, :] = (
            cot_v[rows, :].astype(F32) * up * sig * (1.0 + g * (1.0 - sig))
        ).astype(BF16)

    g_cross(zl).wait_recv()
    up_out[...] = gp[zl, mine, :] + gxr[zl].astype(F32)

    @pl.when(zl > 0)
    def _():
        g_right(zl).wait_recv()
        up_out[...] += grl[zl].astype(F32)

    @pl.when(zl < 3)
    def _():
        g_left(zl).wait_recv()
        up_out[...] += grr[zl].astype(F32)

    @pl.when(jnp.logical_not(self_source))
    def _():
        f_send(0).wait_recv()

    token_out[...] = tgr[...]

    for d in range(1, 4):
        tok_send(d).wait_send()
        s2_copy(d).wait_send()
        t_send(d).wait_send()
    for d in range(1, 8):
        s1_copy(d).wait_send()
        s3_copy(d).wait_send()
    for i in range(3):
        y_right(i).wait_send()
        y_left(i).wait_send()
        p_minus(i).wait_send()
        p_plus(i).wait_send()
    for b in range(4):
        c_send(b).wait_send()
        g_cross(b).wait_send()

        @pl.when(jnp.logical_and(zl < 3, b <= zl))
        def _():
            z_right(b).wait_send()

        @pl.when(jnp.logical_and(zl > 0, b >= zl))
        def _():
            z_left(b).wait_send()

        @pl.when(b > zl)
        def _():
            g_right(b).wait_send()

        @pl.when(b < zl)
        def _():
            g_left(b).wait_send()

    @pl.when(jnp.logical_not(collects))
    def _():
        z_copy.wait_send()

    for j in range(2):
        @pl.when(jnp.logical_and(collects, jnp.logical_not(final_self(j))))
        def _():
            f_send(j).wait_send()


def on_device(tokens, gate_values, up_latent, hidden_grad):
    dma = pltpu.SemaphoreType.DMA
    vm = pltpu.VMEM
    return pl.pallas_call(
        kernel,
        out_shape=(
            jax.ShapeDtypeStruct((TOK, COLS), BF16),
            jax.ShapeDtypeStruct((TOK, COLS), BF16),
            jax.ShapeDtypeStruct((TOK, 512), BF16),
            jax.ShapeDtypeStruct((ROWS, COLS), F32),
        ),
        in_specs=[pl.BlockSpec(memory_space=pl.ANY)] * 4,
        out_specs=(pl.BlockSpec(memory_space=pltpu.VMEM),) * 4,
        scratch_shapes=[
            vm((ROWS, COLS), F32),
            vm((4, 2, ROWS, COLS), BF16),
            vm((BLOCK, COLS), BF16),
            vm((BLOCK, BLOCK), BF16),
            vm((256, BLOCK), BF16),
            vm((BLOCK, COLS), BF16),
            vm((TOK, COLS), BF16),
            vm((TOK, COLS), BF16),
            vm((4, 256, COLS), F32),
            vm((4, ROWS, COLS), BF16),
            vm((4, ROWS, COLS), BF16),
            vm((4, ROWS, COLS), BF16),
            vm((4, ROWS, COLS), BF16),
            vm((4, ROWS, COLS), BF16),
            vm((3, TOK, COLS), F32),
            vm((3, TOK, COLS), BF16),
            vm((TOK, COLS), BF16),
            vm((TOK, COLS), BF16),
            vm((TOK, COLS), BF16),
            vm((TOK, BLOCK), F32),
            vm((3, TOK, BLOCK), BF16),
            vm((3, TOK, BLOCK), BF16),
            vm((TOK, BLOCK), BF16),
            vm((TOK, BLOCK), BF16),
            vm((2, TOK, 512), BF16),
            vm((TOK, 512), BF16),
            vm((8, 8, 128), F32),
            vm((4, 8, 128), F32),
            vm((8, 8, 128), F32),
            dma((4,)),
            dma((4,)), dma((4,)), dma((4,)), dma((4,)), dma((4,)),
            dma((3,)), dma((3,)), dma((3,)), dma((3,)), dma((4,)), dma((4,)),
            dma((8,)), dma((8,)), dma((4,)), dma((4,)), dma((8,)), dma((8,)),
            dma((4,)), dma((4,)), dma((4,)), dma((4,)), dma((4,)), dma((4,)),
            dma((2, 3)), dma((2, 3)), dma((4,)), dma((4,)), dma, dma, dma((2,)), dma,
        ],
        compiler_params=pltpu.CompilerParams(
            collective_id=0, has_side_effects=True, vmem_limit_bytes=60 * 1024 * 1024
        ),
    )(tokens, gate_values, up_latent, hidden_grad)


def solution(mesh):
    placed = (P("dp", None), P("dp", "tensor"), P("dp", "tensor"), P("dp", "tensor"))
    return jax.shard_map(
        on_device,
        mesh=mesh,
        in_specs=placed,
        out_specs=(P("dp", "tensor"), P("dp", "tensor"), P("dp", "tensor"), P("dp", "tensor")),
        check_vma=False,
    )
```

```python
import functools

import jax
import jax.numpy as jnp
from jax import lax
from jax.experimental import pallas as pl
from jax.experimental.pallas import tpu as pltpu
from jax.sharding import PartitionSpec as P

D = 4096
FF = 14336
TOK = 256
COLS = 1792
HALF = COLS // 2
ROWS = 128
BLOCK = 1024
EPSILON = 1e-05
MESH = pl.DeviceIdType.MESH
F32 = jnp.float32
BF16 = jnp.bfloat16


def kernel(
    tokens, gate, latent, cot,
    hidden_out, gate_out, token_out, up_out,
    lat32, wg, wt, tokg, tokt, ucg, gate_v, cot_v, fa, fb,
    gp, gxs, gxr, gsend, grl, grr,
    pvf, pvs, fwd, chain, direct,
    tt_own, tt_send, tt_recv, zsend, zrecv, fsend, tgr,
    s1, s2, s3,
    in_sem, zr_sem, zsr_sem, zsl_sem, cs_sem, cr_sem,
    yrs, yrr, yls, ylr, tks, tkr, txs, txr,
    s1s, s1r, s2s, s2r, s3s, s3r,
    gcs, gcr, gls, glr, grs, grr_sem,
    ops, opr, tts, ttr, zxs, zxr, fs, fr,
):
    me_dp = lax.axis_index("dp")
    me_t = lax.axis_index("tensor")
    y = me_dp // 8
    g8 = me_dp % 8
    zl = g8 // 2
    k = g8 % 2
    x = me_t % 4
    zh = me_t // 4

    def dp_of(yy, zz, kk):
        return yy * 8 + zz * 2 + kk

    def at_y(d):
        return (((y + d) % 4) * 8 + g8, me_t)

    def at_z(zz):
        return (dp_of(y, zz, k), me_t)

    other = (dp_of(y, zl, 1 - k), me_t)

    def at_x(d):
        return (me_dp, zh * 4 + (x + d) % 4)

    flip = (me_dp, (1 - zh) * 4 + x)

    def rcopy(src, dst, ssem, rsem, dev):
        return pltpu.make_async_remote_copy(
            src_ref=src, dst_ref=dst, send_sem=ssem, recv_sem=rsem,
            device_id=dev, device_id_type=MESH,
        )

    source_x, source_y = y, 2 * zh + x // 2
    self_source = jnp.logical_and(source_x == x, source_y == y)
    collects = zh == y // 2

    def final_dev(j):
        return (dp_of(x, zl, k), zh * 4 + 2 * (y % 2) + j)

    def final_self(j):
        return jnp.logical_and(x == y, 2 * (y % 2) + j == x)

    def span(start, size):
        return pl.ds(pl.multiple_of(start, size), size)

    lat_in = pltpu.make_async_copy(latent, lat32, in_sem.at[0])
    gate_in = pltpu.make_async_copy(gate, gate_v, in_sem.at[1])
    cot_in = pltpu.make_async_copy(cot, cot_v, in_sem.at[2])
    tok_in = pltpu.make_async_copy(
        tokens.at[:, span(y * BLOCK, BLOCK)], tokg.at[span(y * TOK, TOK)], in_sem.at[3]
    )
    lat_in.start()
    gate_in.start()
    cot_in.start()
    tok_in.start()

    barrier = pltpu.get_barrier_semaphore()

    def greet(dev):
        pl.semaphore_signal(barrier, inc=1, device_id=dev, device_id_type=MESH)

    for d in range(1, 4):
        greet(at_y(d))
    for d in range(1, 8):
        greet((y * 8 + (g8 + d) % 8, me_t))
        greet((me_dp, (me_t + d) % 8))

    @pl.when(jnp.logical_not(self_source))
    def _():
        greet((dp_of(source_y, zl, k), zh * 4 + source_x))

    takers = jnp.int32(2)
    for j in range(2):
        takers = takers - jnp.where(final_self(j), 1, 0)
    pl.semaphore_wait(barrier, 17 + jnp.where(collects, takers, 0))

    def tok_send(d):
        yy = (y + d) % 4
        return rcopy(
            tokens.at[span(x * 64, 64), span(yy * BLOCK, BLOCK)],
            tokg.at[span(y * TOK + x * 64, 64)],
            tks.at[d], tkr.at[d], at_y(d),
        )

    def tok_share(d, e):
        piece = tokg.at[span(((y + 4 - d) % 4) * TOK + x * 64, 64)]
        return rcopy(piece, piece, txs.at[d, e], txr.at[d, e], at_x(e))

    for d in (1, 3, 2):
        tok_send(d).start()

    lat_in.wait()

    def cast_rows(i, acc):
        rows = span(i * 16, 16)
        half = lat32[rows, :].astype(BF16)
        wg[zl, k, rows, :] = half
        mag = jnp.abs(half.astype(F32))
        mag = mag[0:8] + mag[8:16]
        tot = mag[:, 0:128]
        for c in range(1, COLS // 128):
            tot = tot + mag[:, c * 128:(c + 1) * 128]
        return acc + tot

    part = lax.fori_loop(0, ROWS // 16, cast_rows, jnp.zeros((8, 128), F32))

    def z_right(b):
        return rcopy(wg.at[b, k], wg.at[b, k], zsr_sem.at[b], zr_sem.at[b], at_z(lax.rem(zl + 1, 4)))

    def z_left(b):
        return rcopy(wg.at[b, k], wg.at[b, k], zsl_sem.at[b], zr_sem.at[b], at_z(lax.rem(zl + 3, 4)))

    def c_send(b):
        return rcopy(wg.at[b, k], wg.at[b, k], cs_sem.at[b], cr_sem.at[b], other)

    def c_recv(b):
        return rcopy(wg.at[b, k], wg.at[b, 1 - k], cs_sem.at[b], cr_sem.at[b], other)

    @pl.when(zl < 3)
    def _():
        z_right(zl).start()

    @pl.when(zl > 0)
    def _():
        z_left(zl).start()

    c_send(zl).start()

    s1[g8] = part

    def s1_copy(d):
        return rcopy(s1.at[g8], s1.at[g8], s1s.at[d], s1r.at[d], (y * 8 + (g8 + d) % 8, me_t))

    def s2_copy(d):
        return rcopy(s2.at[y], s2.at[y], s2s.at[d], s2r.at[d], at_y(d))

    def s3_copy(d):
        return rcopy(s3.at[me_t], s3.at[me_t], s3s.at[d], s3r.at[d], (me_dp, (me_t + d) % 8))

    for d in range(1, 8):
        s1_copy(d).start()

    gate_in.wait()
    cot_in.wait()

    def cot_rows(lo, hi):
        @pl.loop(lo // 16, hi // 16)
        def _(i):
            rows = span(i * 16, 16)
            g = gate_v[rows, :].astype(F32)
            act = g * jax.nn.sigmoid(g)
            ucg[span(y * TOK + i * 16, 16), :] = (cot_v[rows, :].astype(F32) * act).astype(BF16)

    def cols(h):
        return pl.ds(h * HALF, HALF)

    def uc_part(yy, rows, h):
        return ucg.at[span((yy % 4) * TOK + rows * 128, 128), cols(h)]

    def y_right(h, i):
        piece = (uc_part(y, 0, h), uc_part(y, 1, h), uc_part(y + 3, 0, h))[i]
        return rcopy(piece, piece, yrs.at[h, i], yrr.at[h, i], at_y(1))

    def y_left(h, i):
        piece = (uc_part(y, 1, h), uc_part(y, 0, h), uc_part(y + 1, 1, h))[i]
        return rcopy(piece, piece, yls.at[h, i], ylr.at[h, i], at_y(3))

    def y_start(h):
        y_right(h, 0).start()
        y_left(h, 0).start()
        y_right(h, 1).start()
        y_left(h, 1).start()

    def y_pass(h):
        y_right(h, 0).wait_recv()
        y_right(h, 2).start()
        y_left(h, 0).wait_recv()
        y_left(h, 2).start()

    def y_wait(h, i):
        y_right(h, i).wait_recv()
        y_left(h, i).wait_recv()

    cot_rows(0, 256)
    y_start(0)

    for d in (1, 3, 2):
        tok_send(d).wait_recv()
        for e in (2, 1, 3):
            tok_share(d, e).start()

    for d in range(1, 8):
        s1_copy(d).wait_recv()
    tot = s1[0]
    for i in range(1, 8):
        tot = tot + s1[i]
    s2[y] = tot
    for d in range(1, 4):
        s2_copy(d).start()

    def at_distance(s, do):
        @pl.when(zl - s >= 0)
        def _():
            do(lax.rem(zl - s + 4, 4), True)

        @pl.when(zl + s <= 3)
        def _():
            do(lax.rem(zl + s, 4), False)

    def z_pass(b, from_left):
        if from_left:
            z_right(b).wait_recv()

            @pl.when(zl < 3)
            def _():
                z_right(b).start()
        else:
            z_left(b).wait_recv()

            @pl.when(zl > 0)
            def _():
                z_left(b).start()

        c_send(b).start()

    y_pass(0)
    y_start(1)
    at_distance(1, z_pass)
    for d in range(1, 4):
        s2_copy(d).wait_recv()
    tot = s2[0]
    for i in range(1, 4):
        tot = tot + s2[i]
    s3[me_t] = tot
    for d in range(1, 8):
        s3_copy(d).start()

    @pl.loop(0, TOK // 16)
    def _(i):
        rows = span(i * 16, 16)
        g = gate_v[rows, :].astype(F32)
        sig = jax.nn.sigmoid(g)
        fa[rows, :] = g * sig
        fb[rows, :] = cot_v[rows, :].astype(F32) * sig * (1.0 + g * (1.0 - sig))

    for d in range(1, 8):
        s3_copy(d).wait_recv()
    tot = s3[0]
    for i in range(1, 8):
        tot = tot + s3[i]
    total = jnp.sum(jnp.sum(tot, axis=0, keepdims=True), axis=1, keepdims=True)
    scale = total / (D * FF) + EPSILON
    bound = 0.5 * scale
    plus = scale.astype(BF16).astype(F32)

    def tern(b, from_left=None):
        c_recv(b).wait_recv()

        @pl.loop(0, 16)
        def _(i):
            wide = wg[b, i // 8, span((i % 8) * 16, 16), :].astype(F32)
            value = jnp.where(wide > bound, plus, jnp.where(wide < -bound, -plus, 0.0))
            wt[span(b * 256 + i * 16, 16), :] = value.astype(BF16)

    def m3(yy, half):
        yy = yy % 4
        d = (yy + 4 - x) % 4
        tt_send[d, half] = lax.dot_general(
            ucg[span(yy * TOK, TOK), :], wt[span(half * 512, 512), :],
            (((1,), (1,)), ((), ())), preferred_element_type=F32,
        ).astype(BF16)

        @pl.when(d > 0)
        def _():
            t_send(d, half).start()

    def t_send(d, half):
        return rcopy(tt_send.at[d, half], tt_recv.at[d, half], tts.at[d, half], ttr.at[d, half], at_x(d))

    early, late = zl // 2, 1 - zl // 2

    tern(zl)
    at_distance(1, tern)
    y_wait(0, 1)
    y_wait(0, 2)
    at_distance(2, z_pass)
    at_distance(2, tern)

    tok_in.wait()
    for d in (1, 3, 2):
        for e in (2, 1, 3):
            tok_share(d, e).wait_recv()
    for b in range(4):
        tokt[b, 0:128, :] = tokg[:, span(b * 256 + k * 128, 128)].T
        tokt[b, 128:256, :] = tokg[:, span(b * 256 + (1 - k) * 128, 128)].T

    def m1(target, h):
        term = jnp.dot(tokt[target], ucg[:, cols(h)], preferred_element_type=F32)
        gp[target, :, cols(h)] = term[0:128]
        gxs[target, :, cols(h)] = term[128:256].astype(BF16)
        g_cross(target, h).start()

    def part_of(ref, target, h):
        return ref.at[target, :, cols(h)]

    def g_cross(target, h):
        return rcopy(part_of(gxs, target, h), part_of(gxr, target, h), gcs.at[target, h], gcr.at[target, h], other)

    def g_right(target, h):
        return rcopy(
            part_of(gsend, target, h), part_of(grl, target, h),
            grs.at[target, h], glr.at[target, h], at_z(lax.rem(zl + 1, 4)),
        )

    def g_left(target, h):
        return rcopy(
            part_of(gsend, target, h), part_of(grr, target, h),
            gls.at[target, h], grr_sem.at[target, h], at_z(lax.rem(zl + 3, 4)),
        )

    def add_up(target, h, extra):
        @pl.loop(0, ROWS // 16)
        def _(i):
            rows = span(i * 16, 16)
            value = gp[target, rows, cols(h)] + gxr[target, rows, cols(h)].astype(F32)
            if extra is not None:
                value = value + extra[target, rows, cols(h)].astype(F32)
            gsend[target, rows, cols(h)] = value.astype(BF16)

    def combine(target, h):
        g_cross(target, h).wait_recv()

        @pl.when(target > zl)
        def _():
            @pl.when(zl == 0)
            def _():
                add_up(target, h, None)

            @pl.when(zl > 0)
            def _():
                g_right(target, h).wait_recv()
                add_up(target, h, grl)

            g_right(target, h).start()

        @pl.when(target < zl)
        def _():
            @pl.when(zl == 3)
            def _():
                add_up(target, h, None)

            @pl.when(zl < 3)
            def _():
                g_left(target, h).wait_recv()
                add_up(target, h, grr)

            g_left(target, h).start()

    def pick(a0, a1, a2, a3):
        return jnp.where(zl == 0, a0, jnp.where(zl == 1, a1, jnp.where(zl == 2, a2, a3)))

    order = [pick(3, 3, 0, 0), pick(2, 0, 3, 1), pick(1, 2, 1, 2), zl]
    edge = jnp.logical_or(zl == 0, zl == 3)

    def m2(yy, first, second):
        term = jnp.dot(tokg[span((yy % 4) * TOK, TOK), :], wt[...], preferred_element_type=F32)
        first[0:128, :] = term[0:128].astype(first.dtype)
        second[128:256, :] = term[128:256].astype(second.dtype)

    A, B = pl.ds(0, 128), pl.ds(128, 128)

    def p_minus(i):
        slot, rows = ((0, A), (1, B), (1, A))[i]
        dst = (fwd, direct, chain)[i]
        return rcopy(pvs.at[slot, rows], dst.at[rows], ops.at[0, i], opr.at[0, i], at_y(3))

    def p_plus(i):
        slot, rows = ((0, B), (2, A), (2, B))[i]
        dst = (fwd, direct, chain)[i]
        return rcopy(pvs.at[slot, rows], dst.at[rows], ops.at[1, i], opr.at[1, i], at_y(1))

    def opposite():
        m2(y + 2, pvs.at[0], pvs.at[0])
        p_minus(0).start()
        p_plus(0).start()

    def ends(i, h):
        @pl.when(edge)
        def _():
            combine(order[i], h)

    def middle(i, h):
        @pl.when(jnp.logical_not(edge))
        def _():
            combine(order[i], h)

    m1(order[0], 0)
    ends(0, 0)
    y_pass(1)
    m1(order[1], 0)
    ends(1, 0)
    m1(order[2], 0)
    ends(2, 0)
    m1(order[3], 0)
    m3(y, early)
    y_wait(1, 1)
    m3(y + 1, early)
    m3(y + 3, early)
    middle(0, 0)
    at_distance(3, z_pass)
    at_distance(3, tern)
    opposite()
    y_wait(1, 2)
    m1(order[0], 1)
    ends(0, 1)
    m3(y + 2, early)
    middle(2, 0)
    m2(y + 3, pvf.at[1], pvs.at[1])
    p_minus(1).start()
    m2(y + 1, pvs.at[2], pvf.at[1])
    p_plus(1).start()
    middle(1, 0)
    m1(order[1], 1)
    ends(1, 1)
    m1(order[2], 1)
    ends(2, 1)
    m1(order[3], 1)
    for d in range(4):
        m3(y + d, late)

    def z_copy(half):
        return rcopy(zsend.at[half], zrecv.at[half], zxs.at[half], zxr.at[half], flip)

    def sum_x(half):
        for d in range(1, 4):
            t_send(d, half).wait_recv()

        @pl.loop(0, TOK // 16)
        def _(i):
            rows = span(i * 16, 16)
            total = tt_send[0, half, rows, :].astype(F32)
            for d in range(1, 4):
                total = total + tt_recv[d, half, rows, :].astype(F32)
            tt_own[half, rows, :] = total
            zsend[half, rows, :] = total.astype(BF16)

        @pl.when(jnp.logical_not(collects))
        def _():
            z_copy(half).start()

    def f_send(half):
        return rcopy(fsend.at[half], tgr, fs.at[half], fr, final_dev(half))

    def sum_z(half):
        @pl.when(collects)
        def _():
            z_copy(half).wait_recv()

            @pl.loop(0, TOK // 16)
            def _(i):
                rows = span(i * 16, 16)
                fsend[half, rows, :] = (tt_own[half, rows, :] + zrecv[half, rows, :].astype(F32)).astype(BF16)

            @pl.when(jnp.logical_not(final_self(half)))
            def _():
                f_send(half).start()

            @pl.when(final_self(half))
            def _():
                tgr[...] = fsend[half]

    sum_x(early)
    middle(0, 1)

    def add_fwd(slot, h):
        @pl.loop(h * 8, h * 8 + 8)
        def _(i):
            rows = span(i * 16, 16)
            pvs[slot, rows, :] = (pvf[1, rows, :] + fwd[rows, :].astype(F32)).astype(BF16)

    p_minus(0).wait_recv()
    add_fwd(1, 0)
    p_minus(2).start()
    p_plus(0).wait_recv()
    add_fwd(2, 1)
    p_plus(2).start()
    m2(y, pvf.at[0], pvf.at[0])
    middle(2, 1)
    middle(1, 1)
    sum_x(late)
    sum_z(early)

    def finish(h):
        @pl.loop(h * 8, h * 8 + 8)
        def _(i):
            rows = span(i * 16, 16)
            up = pvf[0, rows, :] + chain[rows, :].astype(F32) + direct[rows, :].astype(F32)
            hidden_out[rows, :] = (fa[rows, :] * up).astype(BF16)
            gate_out[rows, :] = (fb[rows, :] * up).astype(BF16)

    p_plus(1).wait_recv()
    p_minus(2).wait_recv()
    finish(0)
    p_minus(1).wait_recv()
    p_plus(2).wait_recv()
    finish(1)

    sum_z(late)

    for h in range(2):
        g_cross(zl, h).wait_recv()
        up_out[:, cols(h)] = gp[zl, :, cols(h)] + gxr[zl, :, cols(h)].astype(F32)

        @pl.when(zl > 0)
        def _():
            g_right(zl, h).wait_recv()
            up_out[:, cols(h)] += grl[zl, :, cols(h)].astype(F32)

        @pl.when(zl < 3)
        def _():
            g_left(zl, h).wait_recv()
            up_out[:, cols(h)] += grr[zl, :, cols(h)].astype(F32)

    @pl.when(jnp.logical_not(self_source))
    def _():
        f_send(0).wait_recv()

    token_out[...] = tgr[...]

    for d in range(1, 4):
        tok_send(d).wait_send()
        s2_copy(d).wait_send()
        t_send(d, 0).wait_send()
        t_send(d, 1).wait_send()
        for e in range(1, 4):
            tok_share(d, e).wait_send()
    for d in range(1, 8):
        s1_copy(d).wait_send()
        s3_copy(d).wait_send()
    for i in range(3):
        for h in range(2):
            y_right(h, i).wait_send()
            y_left(h, i).wait_send()
        p_minus(i).wait_send()
        p_plus(i).wait_send()
    for b in range(4):
        c_send(b).wait_send()
        g_cross(b, 0).wait_send()
        g_cross(b, 1).wait_send()

        @pl.when(jnp.logical_and(zl < 3, b <= zl))
        def _():
            z_right(b).wait_send()

        @pl.when(jnp.logical_and(zl > 0, b >= zl))
        def _():
            z_left(b).wait_send()

        @pl.when(b > zl)
        def _():
            g_right(b, 0).wait_send()
            g_right(b, 1).wait_send()

        @pl.when(b < zl)
        def _():
            g_left(b, 0).wait_send()
            g_left(b, 1).wait_send()

    @pl.when(jnp.logical_not(collects))
    def _():
        z_copy(0).wait_send()
        z_copy(1).wait_send()

    for j in range(2):
        @pl.when(jnp.logical_and(collects, jnp.logical_not(final_self(j))))
        def _():
            f_send(j).wait_send()


def on_device(tokens, gate_values, up_latent, hidden_grad):
    dma = pltpu.SemaphoreType.DMA
    vm = pltpu.VMEM
    return pl.pallas_call(
        kernel,
        out_shape=(
            jax.ShapeDtypeStruct((TOK, COLS), BF16),
            jax.ShapeDtypeStruct((TOK, COLS), BF16),
            jax.ShapeDtypeStruct((TOK, 512), BF16),
            jax.ShapeDtypeStruct((ROWS, COLS), F32),
        ),
        in_specs=[pl.BlockSpec(memory_space=pl.ANY)] * 4,
        out_specs=(pl.BlockSpec(memory_space=pltpu.VMEM),) * 4,
        scratch_shapes=[
            vm((ROWS, COLS), F32),
            vm((4, 2, ROWS, COLS), BF16),
            vm((BLOCK, COLS), BF16),
            vm((BLOCK, BLOCK), BF16),
            vm((4, 256, BLOCK), BF16),
            vm((BLOCK, COLS), BF16),
            vm((TOK, COLS), BF16),
            vm((TOK, COLS), BF16),
            vm((TOK, COLS), F32),
            vm((TOK, COLS), F32),
            vm((4, ROWS, COLS), F32),
            vm((4, ROWS, COLS), BF16),
            vm((4, ROWS, COLS), BF16),
            vm((4, ROWS, COLS), BF16),
            vm((4, ROWS, COLS), BF16),
            vm((4, ROWS, COLS), BF16),
            vm((2, TOK, COLS), F32),
            vm((3, TOK, COLS), BF16),
            vm((TOK, COLS), BF16),
            vm((TOK, COLS), BF16),
            vm((TOK, COLS), BF16),
            vm((2, TOK, 512), F32),
            vm((4, 2, TOK, 512), BF16),
            vm((4, 2, TOK, 512), BF16),
            vm((2, TOK, 512), BF16),
            vm((2, TOK, 512), BF16),
            vm((2, TOK, 512), BF16),
            vm((TOK, 512), BF16),
            vm((8, 8, 128), F32),
            vm((4, 8, 128), F32),
            vm((8, 8, 128), F32),
            dma((4,)),
            dma((4,)), dma((4,)), dma((4,)), dma((4,)), dma((4,)),
            dma((2, 3)), dma((2, 3)), dma((2, 3)), dma((2, 3)), dma((4,)), dma((4,)), dma((4, 4)), dma((4, 4)),
            dma((8,)), dma((8,)), dma((4,)), dma((4,)), dma((8,)), dma((8,)),
            dma((4, 2)), dma((4, 2)), dma((4, 2)), dma((4, 2)), dma((4, 2)), dma((4, 2)),
            dma((2, 3)), dma((2, 3)), dma((4, 2)), dma((4, 2)), dma((2,)), dma((2,)), dma((2,)), dma,
        ],
        compiler_params=pltpu.CompilerParams(
            collective_id=0, has_side_effects=True, vmem_limit_bytes=60 * 1024 * 1024
        ),
    )(tokens, gate_values, up_latent, hidden_grad)


def solution(mesh):
    placed = (P("dp", None), P("dp", "tensor"), P("dp", "tensor"), P("dp", "tensor"))
    return jax.shard_map(
        on_device,
        mesh=mesh,
        in_specs=placed,
        out_specs=(P("dp", "tensor"), P("dp", "tensor"), P("dp", "tensor"), P("dp", "tensor")),
        check_vma=False,
    )
```

```python
import functools

import jax
import jax.numpy as jnp
from jax import lax
from jax.experimental import pallas as pl
from jax.experimental.pallas import tpu as pltpu
from jax.sharding import PartitionSpec as P

D = 4096
FF = 14336
TOK = 256
COLS = 1792
HALF = COLS // 2
ROWS = 128
BLOCK = 1024
EPSILON = 1e-05
MESH = pl.DeviceIdType.MESH
F32 = jnp.float32
BF16 = jnp.bfloat16


def kernel(
    tokens, gate, latent, cot,
    hidden_out, gate_out, token_out, up_out,
    lat32, wg, wt, tokg, tokt, ucg, gate_v, cot_v, fa, fb,
    gp, gxs, gxr, gsend, grl, grr,
    pvf, pvs, fwd, chain, direct,
    tt_send, tt_recv, tt_own, zsend, zrecv, fsend, tgr,
    s1, s2, s3,
    in_sem, zr_sem, zsr_sem, zsl_sem, cs_sem, cr_sem,
    yrs, yrr, yls, ylr, tks, tkr, txs, txr,
    s1s, s1r, s2s, s2r, s3s, s3r,
    gcs, gcr, gls, glr, grs, grr_sem,
    ops, opr, tts, ttr, zxs, zxr, fs, fr,
):
    me_dp = lax.axis_index("dp")
    me_t = lax.axis_index("tensor")
    y = me_dp // 8
    g8 = me_dp % 8
    zl = g8 // 2
    k = g8 % 2
    x = me_t % 4
    zh = me_t // 4

    def dp_of(yy, zz, kk):
        return yy * 8 + zz * 2 + kk

    def at_y(d):
        return (((y + d) % 4) * 8 + g8, me_t)

    def at_z(zz):
        return (dp_of(y, zz, k), me_t)

    other = (dp_of(y, zl, 1 - k), me_t)

    def at_x(d):
        return (me_dp, zh * 4 + (x + d) % 4)

    flip = (me_dp, (1 - zh) * 4 + x)

    def rcopy(src, dst, ssem, rsem, dev):
        return pltpu.make_async_remote_copy(
            src_ref=src, dst_ref=dst, send_sem=ssem, recv_sem=rsem,
            device_id=dev, device_id_type=MESH,
        )

    source_y = 2 * zh + x // 2
    collects = zh == y // 2

    def final_dev(yy, half):
        return (dp_of(yy, zl, k), zh * 4 + 2 * (y % 2) + half)

    def final_self(yy, half):
        return jnp.logical_and(yy == y, 2 * (y % 2) + half == x)

    def source_self(xx):
        return jnp.logical_and(source_y == y, xx == x)

    def span(start, size):
        return pl.ds(pl.multiple_of(start, size), size)

    lat_in = pltpu.make_async_copy(latent, lat32, in_sem.at[0])
    gate_in = pltpu.make_async_copy(gate, gate_v, in_sem.at[1])
    cot_in = pltpu.make_async_copy(cot, cot_v, in_sem.at[2])
    tok_in = pltpu.make_async_copy(
        tokens.at[:, span(y * BLOCK, BLOCK)], tokg.at[span(y * TOK, TOK)], in_sem.at[3]
    )
    lat_in.start()
    gate_in.start()
    cot_in.start()
    tok_in.start()

    barrier = pltpu.get_barrier_semaphore()

    def greet(dev):
        pl.semaphore_signal(barrier, inc=1, device_id=dev, device_id_type=MESH)

    for d in range(1, 4):
        greet(at_y(d))
    for d in range(1, 8):
        greet((y * 8 + (g8 + d) % 8, me_t))
        greet((me_dp, (me_t + d) % 8))

    for xx in range(4):
        @pl.when(jnp.logical_not(source_self(xx)))
        def _():
            greet((dp_of(source_y, zl, k), zh * 4 + xx))

    takers = jnp.int32(8)
    for yy in range(4):
        for half in range(2):
            takers = takers - jnp.where(final_self(yy, half), 1, 0)
    pl.semaphore_wait(barrier, 17 + jnp.where(collects, takers, 0))

    def tok_send(d):
        yy = (y + d) % 4
        return rcopy(
            tokens.at[span(x * 64, 64), span(yy * BLOCK, BLOCK)],
            tokg.at[span(y * TOK + x * 64, 64)],
            tks.at[d], tkr.at[d], at_y(d),
        )

    def tok_share(d, e):
        piece = tokg.at[span(((y + 4 - d) % 4) * TOK + x * 64, 64)]
        return rcopy(piece, piece, txs.at[d, e], txr.at[d, e], at_x(e))

    for d in (1, 3, 2):
        tok_send(d).start()

    lat_in.wait()

    def cast_rows(i, acc):
        rows = span(i * 16, 16)
        half = lat32[rows, :].astype(BF16)
        wg[zl, k, rows, :] = half
        mag = jnp.abs(half.astype(F32))
        mag = mag[0:8] + mag[8:16]
        tot = mag[:, 0:128]
        for c in range(1, COLS // 128):
            tot = tot + mag[:, c * 128:(c + 1) * 128]
        return acc + tot

    part = lax.fori_loop(0, ROWS // 16, cast_rows, jnp.zeros((8, 128), F32))

    def z_right(b):
        return rcopy(wg.at[b, k], wg.at[b, k], zsr_sem.at[b], zr_sem.at[b], at_z(lax.rem(zl + 1, 4)))

    def z_left(b):
        return rcopy(wg.at[b, k], wg.at[b, k], zsl_sem.at[b], zr_sem.at[b], at_z(lax.rem(zl + 3, 4)))

    def c_send(b):
        return rcopy(wg.at[b, k], wg.at[b, k], cs_sem.at[b], cr_sem.at[b], other)

    def c_recv(b):
        return rcopy(wg.at[b, k], wg.at[b, 1 - k], cs_sem.at[b], cr_sem.at[b], other)

    s1[g8] = part

    def s1_copy(d):
        return rcopy(s1.at[g8], s1.at[g8], s1s.at[d], s1r.at[d], (y * 8 + (g8 + d) % 8, me_t))

    def s2_copy(d):
        return rcopy(s2.at[y], s2.at[y], s2s.at[d], s2r.at[d], at_y(d))

    def s3_copy(d):
        return rcopy(s3.at[me_t], s3.at[me_t], s3s.at[d], s3r.at[d], (me_dp, (me_t + d) % 8))

    for d in range(1, 8):
        s1_copy(d).start()

    @pl.when(zl < 3)
    def _():
        z_right(zl).start()

    @pl.when(zl > 0)
    def _():
        z_left(zl).start()

    c_send(zl).start()


    gate_in.wait()
    cot_in.wait()

    def cot_rows(lo, hi):
        @pl.loop(lo // 16, hi // 16)
        def _(i):
            rows = span(i * 16, 16)
            g = gate_v[rows, :].astype(F32)
            act = g * jax.nn.sigmoid(g)
            ucg[span(y * TOK + i * 16, 16), :] = (cot_v[rows, :].astype(F32) * act).astype(BF16)

    def cols(h):
        return pl.ds(h * HALF, HALF)

    def uc_part(yy, rows, h):
        return ucg.at[span((yy % 4) * TOK + rows * 128, 128), cols(h)]

    def y_right(h, i):
        piece = (uc_part(y, 0, h), uc_part(y, 1, h), uc_part(y + 3, 0, h))[i]
        return rcopy(piece, piece, yrs.at[h, i], yrr.at[h, i], at_y(1))

    def y_left(h, i):
        piece = (uc_part(y, 1, h), uc_part(y, 0, h), uc_part(y + 1, 1, h))[i]
        return rcopy(piece, piece, yls.at[h, i], ylr.at[h, i], at_y(3))

    def y_start(h):
        y_right(h, 0).start()
        y_left(h, 0).start()
        y_right(h, 1).start()
        y_left(h, 1).start()

    def y_pass(h):
        y_right(h, 0).wait_recv()
        y_right(h, 2).start()
        y_left(h, 0).wait_recv()
        y_left(h, 2).start()

    def y_wait(h, i):
        y_right(h, i).wait_recv()
        y_left(h, i).wait_recv()

    cot_rows(0, 256)
    y_start(0)

    def reduced(slots, copy, n):
        for d in range(1, n):
            copy(d).wait_recv()
        tot = slots[0]
        for i in range(1, n):
            tot = tot + slots[i]
        return tot

    s2[y] = reduced(s1, s1_copy, 8)
    for d in range(1, 4):
        s2_copy(d).start()

    @pl.loop(0, TOK // 16)
    def _(i):
        rows = span(i * 16, 16)
        g = gate_v[rows, :].astype(F32)
        sig = jax.nn.sigmoid(g)
        fa[rows, :] = g * sig
        fb[rows, :] = cot_v[rows, :].astype(F32) * sig * (1.0 + g * (1.0 - sig))

    for d in (1, 3, 2):
        tok_send(d).wait_recv()
        for e in (2, 1, 3):
            tok_share(d, e).start()

    def at_distance(s, do):
        @pl.when(zl - s >= 0)
        def _():
            do(lax.rem(zl - s + 4, 4), True)

        @pl.when(zl + s <= 3)
        def _():
            do(lax.rem(zl + s, 4), False)

    def z_pass(b, from_left):
        if from_left:
            z_right(b).wait_recv()

            @pl.when(zl < 3)
            def _():
                z_right(b).start()
        else:
            z_left(b).wait_recv()

            @pl.when(zl > 0)
            def _():
                z_left(b).start()

        c_send(b).start()

    at_distance(1, z_pass)
    y_pass(0)
    y_start(1)
    s3[me_t] = reduced(s2, s2_copy, 4)
    for d in range(1, 8):
        s3_copy(d).start()
    at_distance(2, z_pass)
    def turn(target):
        tokt[target, 0:128, :] = tokg[:, span(target * 256 + k * 128, 128)].T
        tokt[target, 128:256, :] = tokg[:, span(target * 256 + (1 - k) * 128, 128)].T

    y_wait(0, 1)
    y_wait(0, 2)
    tok_in.wait()
    for d in (1, 3, 2):
        for e in (2, 1, 3):
            tok_share(d, e).wait_recv()

    def m1(target, h):
        term = jnp.dot(tokt[target], ucg[:, cols(h)], preferred_element_type=F32)
        gp[target, :, cols(h)] = term[0:128]
        gxs[target, :, cols(h)] = term[128:256].astype(BF16)
        g_cross(target, h).start()

    def part_of(ref, target, h):
        return ref.at[target, :, cols(h)]

    def g_cross(target, h):
        return rcopy(part_of(gxs, target, h), part_of(gxr, target, h), gcs.at[target, h], gcr.at[target, h], other)

    def g_right(target, h):
        return rcopy(
            part_of(gsend, target, h), part_of(grl, target, h),
            grs.at[target, h], glr.at[target, h], at_z(lax.rem(zl + 1, 4)),
        )

    def g_left(target, h):
        return rcopy(
            part_of(gsend, target, h), part_of(grr, target, h),
            gls.at[target, h], grr_sem.at[target, h], at_z(lax.rem(zl + 3, 4)),
        )

    def add_up(target, h, extra):
        @pl.loop(0, ROWS // 16)
        def _(i):
            rows = span(i * 16, 16)
            value = gp[target, rows, cols(h)] + gxr[target, rows, cols(h)].astype(F32)
            if extra is not None:
                value = value + extra[target, rows, cols(h)].astype(F32)
            gsend[target, rows, cols(h)] = value.astype(BF16)

    def combine(target, h):
        g_cross(target, h).wait_recv()

        @pl.when(target > zl)
        def _():
            @pl.when(zl == 0)
            def _():
                add_up(target, h, None)

            @pl.when(zl > 0)
            def _():
                g_right(target, h).wait_recv()
                add_up(target, h, grl)

            g_right(target, h).start()

        @pl.when(target < zl)
        def _():
            @pl.when(zl == 3)
            def _():
                add_up(target, h, None)

            @pl.when(zl < 3)
            def _():
                g_left(target, h).wait_recv()
                add_up(target, h, grr)

            g_left(target, h).start()

    def pick(a0, a1, a2, a3):
        return jnp.where(zl == 0, a0, jnp.where(zl == 1, a1, jnp.where(zl == 2, a2, a3)))

    order = [pick(3, 3, 0, 0), pick(2, 2, 1, 1), pick(1, 0, 3, 2), zl]
    edge = jnp.logical_or(zl == 0, zl == 3)

    def m2(yy, first, second):
        term = jnp.dot(tokg[span((yy % 4) * TOK, TOK), :], wt[...], preferred_element_type=F32)
        first[0:128, :] = term[0:128].astype(first.dtype)
        second[128:256, :] = term[128:256].astype(second.dtype)

    A, B = pl.ds(0, 128), pl.ds(128, 128)

    def p_minus(i):
        slot, rows = ((0, A), (1, B), (1, A))[i]
        dst = (fwd, direct, chain)[i]
        return rcopy(pvs.at[slot, rows], dst.at[rows], ops.at[0, i], opr.at[0, i], at_y(3))

    def p_plus(i):
        slot, rows = ((0, B), (2, A), (2, B))[i]
        dst = (fwd, direct, chain)[i]
        return rcopy(pvs.at[slot, rows], dst.at[rows], ops.at[1, i], opr.at[1, i], at_y(1))

    def opposite():
        m2(y + 2, pvs.at[0], pvs.at[0])
        p_minus(0).start()
        p_plus(0).start()

    def ends(i, h):
        @pl.when(edge)
        def _():
            combine(order[i], h)

    def middle(i, h):
        @pl.when(jnp.logical_not(edge))
        def _():
            combine(order[i], h)

    turn(order[0])
    m1(order[0], 0)
    turn(order[1])
    m1(order[1], 0)
    ends(0, 0)
    y_pass(1)
    turn(order[2])
    m1(order[2], 0)
    ends(1, 0)
    turn(order[3])
    m1(order[3], 0)
    ends(2, 0)

    tot = reduced(s3, s3_copy, 8)
    total = jnp.sum(jnp.sum(tot, axis=0, keepdims=True), axis=1, keepdims=True)
    scale = total / (D * FF) + EPSILON
    bound = 0.5 * scale
    plus = scale.astype(BF16).astype(F32)

    def tern(b, from_left=None):
        c_recv(b).wait_recv()

        @pl.loop(0, 16)
        def _(i):
            wide = wg[b, i // 8, span((i % 8) * 16, 16), :].astype(F32)
            value = jnp.where(wide > bound, plus, jnp.where(wide < -bound, -plus, 0.0))
            wt[span(b * 256 + i * 16, 16), :] = value.astype(BF16)

    def m3(yy, half):
        yy = yy % 4
        tt_send[half, yy] = lax.dot_general(
            ucg[span(yy * TOK, TOK), :], wt[span(half * 512, 512), :],
            (((1,), (1,)), ((), ())), preferred_element_type=F32,
        ).astype(BF16)
        for d in (2, 1, 3):
            t_send(yy, d, half).start()

    def t_send(yy, d, half):
        return rcopy(
            tt_send.at[half, yy, span(((x + d) % 4) * 64, 64)], tt_recv.at[half, yy, d],
            tts.at[half, yy, d], ttr.at[half, yy, d], at_x(d),
        )

    early, late = zl // 2, 1 - zl // 2

    tern(zl)
    at_distance(1, tern)
    at_distance(2, tern)
    at_distance(3, z_pass)
    m3(y, early)
    y_wait(1, 1)
    m3(y + 1, early)
    m3(y + 3, early)
    at_distance(3, tern)
    opposite()
    m3(y, late)
    m3(y + 1, late)
    m3(y + 3, late)
    middle(0, 0)
    y_wait(1, 2)
    m3(y + 2, early)
    m3(y + 2, late)
    m1(order[0], 1)
    m2(y + 3, pvf.at[1], pvs.at[1])
    p_minus(1).start()
    ends(0, 1)
    m2(y + 1, pvs.at[2], pvf.at[1])
    p_plus(1).start()
    middle(1, 0)
    m1(order[1], 1)
    m1(order[2], 1)
    ends(1, 1)
    middle(2, 0)

    def z_copy(half):
        return rcopy(zsend.at[half], zrecv.at[half], zxs.at[half], zxr.at[half], flip)

    def f_send(yy, half):
        return rcopy(fsend.at[half, yy], tgr.at[span(x * 64, 64)], fs.at[half, yy], fr.at[x], final_dev(yy, half))

    def f_recv(xx):
        return rcopy(fsend.at[0, 0], tgr.at[span(xx * 64, 64)], fs.at[0, 0], fr.at[xx], final_dev(0, 0))

    def sum_x(half):
        for i in (0, 1, 3, 2):
            yy = (y + i) % 4
            for d in range(1, 4):
                t_send(yy, d, half).wait_recv()

            @pl.loop(0, 4)
            def _(r):
                rows = span(r * 16, 16)
                total = tt_send[half, yy, span(x * 64 + r * 16, 16), :].astype(F32)
                for d in range(1, 4):
                    total = total + tt_recv[half, yy, d, rows, :].astype(F32)
                tt_own[half, yy, rows, :] = total
                zsend[half, yy, rows, :] = total.astype(BF16)

        @pl.when(jnp.logical_not(collects))
        def _():
            z_copy(half).start()

    def sum_z(half):
        @pl.when(collects)
        def _():
            z_copy(half).wait_recv()
            for yy in range(4):
                fsend[half, yy] = (tt_own[half, yy] + zrecv[half, yy].astype(F32)).astype(BF16)

                @pl.when(jnp.logical_not(final_self(yy, half)))
                def _():
                    f_send(yy, half).start()

                @pl.when(final_self(yy, half))
                def _():
                    tgr[span(x * 64, 64), :] = fsend[half, yy]

    def add_fwd(slot, h):
        @pl.loop(h * 8, h * 8 + 8)
        def _(i):
            rows = span(i * 16, 16)
            pvs[slot, rows, :] = (pvf[1, rows, :] + fwd[rows, :].astype(F32)).astype(BF16)

    sum_x(early)
    ends(2, 1)
    m1(order[3], 1)
    p_minus(0).wait_recv()
    add_fwd(1, 0)
    p_minus(2).start()
    p_plus(0).wait_recv()
    add_fwd(2, 1)
    p_plus(2).start()
    middle(0, 1)
    sum_x(late)
    m2(y, pvf.at[0], pvf.at[0])
    middle(1, 1)
    sum_z(early)
    middle(2, 1)
    sum_z(late)

    def finish(h):
        @pl.loop(h * 8, h * 8 + 8)
        def _(i):
            rows = span(i * 16, 16)
            up = pvf[0, rows, :] + chain[rows, :].astype(F32) + direct[rows, :].astype(F32)
            hidden_out[rows, :] = (fa[rows, :] * up).astype(BF16)
            gate_out[rows, :] = (fb[rows, :] * up).astype(BF16)

    p_plus(1).wait_recv()
    p_minus(2).wait_recv()
    finish(0)
    p_minus(1).wait_recv()
    p_plus(2).wait_recv()
    finish(1)

    for h in range(2):
        g_cross(zl, h).wait_recv()
        up_out[:, cols(h)] = gp[zl, :, cols(h)] + gxr[zl, :, cols(h)].astype(F32)

        @pl.when(zl > 0)
        def _():
            g_right(zl, h).wait_recv()
            up_out[:, cols(h)] += grl[zl, :, cols(h)].astype(F32)

        @pl.when(zl < 3)
        def _():
            g_left(zl, h).wait_recv()
            up_out[:, cols(h)] += grr[zl, :, cols(h)].astype(F32)

    for xx in range(4):
        @pl.when(jnp.logical_not(source_self(xx)))
        def _():
            f_recv(xx).wait_recv()

    token_out[...] = tgr[...]

    for d in range(1, 4):
        tok_send(d).wait_send()
        s2_copy(d).wait_send()
        for b in range(4):
            t_send(b, d, 0).wait_send()
            t_send(b, d, 1).wait_send()
        for e in range(1, 4):
            tok_share(d, e).wait_send()
    for d in range(1, 8):
        s1_copy(d).wait_send()
        s3_copy(d).wait_send()
    for i in range(3):
        for h in range(2):
            y_right(h, i).wait_send()
            y_left(h, i).wait_send()
        p_minus(i).wait_send()
        p_plus(i).wait_send()
    for b in range(4):
        c_send(b).wait_send()
        g_cross(b, 0).wait_send()
        g_cross(b, 1).wait_send()

        @pl.when(jnp.logical_and(zl < 3, b <= zl))
        def _():
            z_right(b).wait_send()

        @pl.when(jnp.logical_and(zl > 0, b >= zl))
        def _():
            z_left(b).wait_send()

        @pl.when(b > zl)
        def _():
            g_right(b, 0).wait_send()
            g_right(b, 1).wait_send()

        @pl.when(b < zl)
        def _():
            g_left(b, 0).wait_send()
            g_left(b, 1).wait_send()

    for half in range(2):
        @pl.when(jnp.logical_not(collects))
        def _():
            z_copy(half).wait_send()

        for yy in range(4):
            @pl.when(jnp.logical_and(collects, jnp.logical_not(final_self(yy, half))))
            def _():
                f_send(yy, half).wait_send()


def on_device(tokens, gate_values, up_latent, hidden_grad):
    dma = pltpu.SemaphoreType.DMA
    vm = pltpu.VMEM
    return pl.pallas_call(
        kernel,
        out_shape=(
            vm((TOK, COLS), BF16),
            vm((TOK, COLS), BF16),
            vm((TOK, 512), BF16),
            vm((ROWS, COLS), F32),
        ),
        in_specs=[pl.BlockSpec(memory_space=pl.ANY)] * 4,
        out_specs=(pl.BlockSpec(memory_space=pltpu.VMEM),) * 4,
        scratch_shapes=[
            vm((ROWS, COLS), F32),
            vm((4, 2, ROWS, COLS), BF16),
            vm((BLOCK, COLS), BF16),
            vm((BLOCK, BLOCK), BF16),
            vm((4, 256, BLOCK), BF16),
            vm((BLOCK, COLS), BF16),
            vm((TOK, COLS), BF16),
            vm((TOK, COLS), BF16),
            vm((TOK, COLS), F32),
            vm((TOK, COLS), F32),
            vm((4, ROWS, COLS), F32),
            vm((4, ROWS, COLS), BF16),
            vm((4, ROWS, COLS), BF16),
            vm((4, ROWS, COLS), BF16),
            vm((4, ROWS, COLS), BF16),
            vm((4, ROWS, COLS), BF16),
            vm((2, TOK, COLS), F32),
            vm((3, TOK, COLS), BF16),
            vm((TOK, COLS), BF16),
            vm((TOK, COLS), BF16),
            vm((TOK, COLS), BF16),
            vm((2, 4, TOK, 512), BF16),
            vm((2, 4, 4, 64, 512), BF16),
            vm((2, 4, 64, 512), F32),
            vm((2, 4, 64, 512), BF16),
            vm((2, 4, 64, 512), BF16),
            vm((2, 4, 64, 512), BF16),
            vm((TOK, 512), BF16),
            vm((8, 8, 128), F32),
            vm((4, 8, 128), F32),
            vm((8, 8, 128), F32),
            dma((4,)),
            dma((4,)), dma((4,)), dma((4,)), dma((4,)), dma((4,)),
            dma((2, 3)), dma((2, 3)), dma((2, 3)), dma((2, 3)), dma((4,)), dma((4,)), dma((4, 4)), dma((4, 4)),
            dma((8,)), dma((8,)), dma((4,)), dma((4,)), dma((8,)), dma((8,)),
            dma((4, 2)), dma((4, 2)), dma((4, 2)), dma((4, 2)), dma((4, 2)), dma((4, 2)),
            dma((2, 3)), dma((2, 3)), dma((2, 4, 4)), dma((2, 4, 4)), dma((2,)), dma((2,)), dma((2, 4)), dma((4,)),
        ],
        compiler_params=pltpu.CompilerParams(
            collective_id=0, has_side_effects=True, vmem_limit_bytes=60 * 1024 * 1024
        ),
    )(tokens, gate_values, up_latent, hidden_grad)


def solution(mesh):
    placed = (P("dp", None), P("dp", "tensor"), P("dp", "tensor"), P("dp", "tensor"))
    return jax.shard_map(
        on_device,
        mesh=mesh,
        in_specs=placed,
        out_specs=(P("dp", "tensor"), P("dp", "tensor"), P("dp", "tensor"), P("dp", "tensor")),
        check_vma=False,
    )
```

```python
import functools

import jax
import jax.numpy as jnp
from jax import lax
from jax.experimental import pallas as pl
from jax.experimental.pallas import tpu as pltpu
from jax.sharding import PartitionSpec as P

D = 4096
FF = 14336
TOK = 256
COLS = 1792
PARTS = ((0, 512), (512, 640), (1152, 640))
ROWS = 128
BLOCK = 1024
EPSILON = 1e-05
MESH = pl.DeviceIdType.MESH
F32 = jnp.float32
BF16 = jnp.bfloat16


def kernel(
    tokens, gate, latent, cot,
    hidden_out, gate_out, token_out, up_out,
    lat32, wg, wt, tokg, tokt, ucg, gate_v, cot_v, fa, fb,
    gp, gxs, gxr, gsend, grl, grr,
    pvf, pvs, fwd, chain, direct,
    tt_send, tt_recv, zrecv, fsend, tgr,
    s1, s2, s3,
    in_sem, zr_sem, zsr_sem, zsl_sem, cs_sem, cr_sem,
    yrs, yrr, yls, ylr, tks, tkr, txs, txr,
    s1s, s1r, s2s, s2r, s3s, s3r,
    gcs, gcr, gls, glr, grs, grr_sem,
    ops, opr, tts, ttr, zxs, zxr, fs, fr,
):
    me_dp = lax.axis_index("dp")
    me_t = lax.axis_index("tensor")
    y = me_dp // 8
    g8 = me_dp % 8
    zl = g8 // 2
    k = g8 % 2
    x = me_t % 4
    zh = me_t // 4

    def dp_of(yy, zz, kk):
        return yy * 8 + zz * 2 + kk

    def at_y(d):
        return (((y + d) % 4) * 8 + g8, me_t)

    def at_z(zz):
        return (dp_of(y, zz, k), me_t)

    other = (dp_of(y, zl, 1 - k), me_t)

    def at_x(d):
        return (me_dp, zh * 4 + (x + d) % 4)

    flip = (me_dp, (1 - zh) * 4 + x)

    def rcopy(src, dst, ssem, rsem, dev):
        return pltpu.make_async_remote_copy(
            src_ref=src, dst_ref=dst, send_sem=ssem, recv_sem=rsem,
            device_id=dev, device_id_type=MESH,
        )

    def final_dev(yy, j):
        return (dp_of(yy, zl, k), zh * 4 + 2 * (y % 2) + j)

    def final_self(yy, j):
        return jnp.logical_and(yy == y, 2 * (y % 2) + j == x)

    def source_self(z, xx):
        return jnp.logical_and(x // 2 + 2 * z == y, xx == x)

    def span(start, size):
        return pl.ds(pl.multiple_of(start, size), size)

    lat_in = pltpu.make_async_copy(latent, lat32, in_sem.at[0])
    gate_in = pltpu.make_async_copy(gate, gate_v, in_sem.at[1])
    cot_in = pltpu.make_async_copy(cot, cot_v, in_sem.at[2])
    tok_in = pltpu.make_async_copy(
        tokens.at[:, span(y * BLOCK, BLOCK)], tokg.at[span(y * TOK, TOK)], in_sem.at[3]
    )
    lat_in.start()
    gate_in.start()
    cot_in.start()
    tok_in.start()

    barrier = pltpu.get_barrier_semaphore()

    def greet(dev):
        pl.semaphore_signal(barrier, inc=1, device_id=dev, device_id_type=MESH)

    for d in range(1, 4):
        greet(at_y(d))
    for d in range(1, 8):
        greet((y * 8 + (g8 + d) % 8, me_t))
        greet((me_dp, (me_t + d) % 8))

    for z in range(2):
        for xx in range(4):
            @pl.when(jnp.logical_not(source_self(z, xx)))
            def _():
                greet((dp_of(x // 2 + 2 * z, zl, k), zh * 4 + xx))

    takers = jnp.int32(8)
    for yy in range(4):
        for j in range(2):
            takers = takers - jnp.where(final_self(yy, j), 1, 0)
    pl.semaphore_wait(barrier, 17 + takers)

    def tok_send(d):
        yy = (y + d) % 4
        return rcopy(
            tokens.at[span(x * 64, 64), span(yy * BLOCK, BLOCK)],
            tokg.at[span(y * TOK + x * 64, 64)],
            tks.at[d], tkr.at[d], at_y(d),
        )

    def tok_share(d, e, c):
        half = zl // 2 if c else 1 - zl // 2
        piece = tokg.at[span(((y + 4 - d) % 4) * TOK + x * 64, 64), span(half * 512, 512)]
        return rcopy(piece, piece, txs.at[d - 1, e - 1, c], txr.at[d - 1, e - 1, c], at_x(e))

    for d in (1, 3, 2):
        tok_send(d).start()

    lat_in.wait()

    def cast_rows(i, acc):
        rows = span(i * 16, 16)
        half = lat32[rows, :].astype(BF16)
        wg[zl, k, rows, :] = half
        mag = jnp.abs(half.astype(F32))
        mag = mag[0:8] + mag[8:16]
        tot = mag[:, 0:128]
        for c in range(1, COLS // 128):
            tot = tot + mag[:, c * 128:(c + 1) * 128]
        return acc + tot

    part = lax.fori_loop(0, ROWS // 16, cast_rows, jnp.zeros((8, 128), F32))

    def z_right(b):
        return rcopy(wg.at[b, k], wg.at[b, k], zsr_sem.at[b], zr_sem.at[b], at_z(lax.rem(zl + 1, 4)))

    def z_left(b):
        return rcopy(wg.at[b, k], wg.at[b, k], zsl_sem.at[b], zr_sem.at[b], at_z(lax.rem(zl + 3, 4)))

    def c_send(b):
        return rcopy(wg.at[b, k], wg.at[b, k], cs_sem.at[b], cr_sem.at[b], other)

    def c_recv(b):
        return rcopy(wg.at[b, k], wg.at[b, 1 - k], cs_sem.at[b], cr_sem.at[b], other)

    s1[g8] = part

    def s1_copy(d):
        return rcopy(s1.at[g8], s1.at[g8], s1s.at[d], s1r.at[d], (y * 8 + (g8 + d) % 8, me_t))

    def s2_copy(d):
        return rcopy(s2.at[y], s2.at[y], s2s.at[d], s2r.at[d], at_y(d))

    def s3_copy(d):
        return rcopy(s3.at[me_t], s3.at[me_t], s3s.at[d], s3r.at[d], (me_dp, (me_t + d) % 8))

    for d in range(1, 8):
        s1_copy(d).start()

    @pl.when(zl < 3)
    def _():
        z_right(zl).start()

    @pl.when(zl > 0)
    def _():
        z_left(zl).start()

    c_send(zl).start()


    gate_in.wait()
    cot_in.wait()

    def cot_rows(lo, hi):
        @pl.loop(lo // 16, hi // 16)
        def _(i):
            rows = span(i * 16, 16)
            g = gate_v[rows, :].astype(F32)
            act = g * jax.nn.sigmoid(g)
            ucg[span(y * TOK + i * 16, 16), :] = (cot_v[rows, :].astype(F32) * act).astype(BF16)

    def cols(h):
        return pl.ds(*PARTS[h])

    def uc_part(yy, rows, h):
        return ucg.at[span((yy % 4) * TOK + rows * 128, 128), cols(h)]

    def y_right(h, i):
        piece = (uc_part(y, 0, h), uc_part(y, 1, h), uc_part(y + 3, 0, h))[i]
        return rcopy(piece, piece, yrs.at[h, i], yrr.at[h, i], at_y(1))

    def y_left(h, i):
        piece = (uc_part(y, 1, h), uc_part(y, 0, h), uc_part(y + 1, 1, h))[i]
        return rcopy(piece, piece, yls.at[h, i], ylr.at[h, i], at_y(3))

    def y_start(h):
        y_right(h, 0).start()
        y_left(h, 0).start()
        y_right(h, 1).start()
        y_left(h, 1).start()

    def y_pass(h):
        y_right(h, 0).wait_recv()
        y_right(h, 2).start()
        y_left(h, 0).wait_recv()
        y_left(h, 2).start()

    def y_wait(h, i):
        y_right(h, i).wait_recv()
        y_left(h, i).wait_recv()

    cot_rows(0, 256)
    y_start(0)

    def reduced(slots, copy, n):
        for d in range(1, n):
            copy(d).wait_recv()
        tot = slots[0]
        for i in range(1, n):
            tot = tot + slots[i]
        return tot

    s2[y] = reduced(s1, s1_copy, 8)
    for d in range(1, 4):
        s2_copy(d).start()

    @pl.loop(0, TOK // 16)
    def _(i):
        rows = span(i * 16, 16)
        g = gate_v[rows, :].astype(F32)
        sig = jax.nn.sigmoid(g)
        fa[rows, :] = g * sig
        fb[rows, :] = cot_v[rows, :].astype(F32) * sig * (1.0 + g * (1.0 - sig))

    for d in (1, 3, 2):
        tok_send(d).wait_recv()
        for e in (2, 1, 3):
            tok_share(d, e, 0).start()
    for d in (1, 3, 2):
        for e in (2, 1, 3):
            tok_share(d, e, 1).start()

    def at_distance(s, do):
        @pl.when(zl - s >= 0)
        def _():
            do(lax.rem(zl - s + 4, 4), True)

        @pl.when(zl + s <= 3)
        def _():
            do(lax.rem(zl + s, 4), False)

    def z_pass(b, from_left):
        if from_left:
            z_right(b).wait_recv()

            @pl.when(zl < 3)
            def _():
                z_right(b).start()
        else:
            z_left(b).wait_recv()

            @pl.when(zl > 0)
            def _():
                z_left(b).start()

        c_send(b).start()

    at_distance(1, z_pass)
    y_pass(0)
    y_start(1)
    def turn(target):
        tokt[target, 0:128, :] = tokg[:, span(target * 256 + k * 128, 128)].T
        tokt[target, 128:256, :] = tokg[:, span(target * 256 + (1 - k) * 128, 128)].T

    def tok_wait(c):
        for d in (1, 3, 2):
            for e in (2, 1, 3):
                tok_share(d, e, c).wait_recv()

    def m1(target, h):
        term = jnp.dot(tokt[target], ucg[:, cols(h)], preferred_element_type=F32)
        gp[target, :, cols(h)] = term[0:128]
        gxs[target, :, cols(h)] = term[128:256].astype(BF16)
        g_cross(target, h).start()

    def part_of(ref, target, h):
        return ref.at[target, :, cols(h)]

    def g_cross(target, h):
        return rcopy(part_of(gxs, target, h), part_of(gxr, target, h), gcs.at[target, h], gcr.at[target, h], other)

    def g_right(target, h):
        return rcopy(
            part_of(gsend, target, h), part_of(grl, target, h),
            grs.at[target, h], glr.at[target, h], at_z(lax.rem(zl + 1, 4)),
        )

    def g_left(target, h):
        return rcopy(
            part_of(gsend, target, h), part_of(grr, target, h),
            gls.at[target, h], grr_sem.at[target, h], at_z(lax.rem(zl + 3, 4)),
        )

    def add_up(target, h, extra):
        @pl.loop(0, ROWS // 16)
        def _(i):
            rows = span(i * 16, 16)
            value = gp[target, rows, cols(h)] + gxr[target, rows, cols(h)].astype(F32)
            if extra is not None:
                value = value + extra[target, rows, cols(h)].astype(F32)
            gsend[target, rows, cols(h)] = value.astype(BF16)

    def combine(target, h):
        g_cross(target, h).wait_recv()

        @pl.when(target > zl)
        def _():
            @pl.when(zl == 0)
            def _():
                add_up(target, h, None)

            @pl.when(zl > 0)
            def _():
                g_right(target, h).wait_recv()
                add_up(target, h, grl)

            g_right(target, h).start()

        @pl.when(target < zl)
        def _():
            @pl.when(zl == 3)
            def _():
                add_up(target, h, None)

            @pl.when(zl < 3)
            def _():
                g_left(target, h).wait_recv()
                add_up(target, h, grr)

            g_left(target, h).start()

    def pick(a0, a1, a2, a3):
        return jnp.where(zl == 0, a0, jnp.where(zl == 1, a1, jnp.where(zl == 2, a2, a3)))

    order = [pick(3, 3, 0, 0), pick(2, 2, 1, 1), pick(1, 0, 3, 2), zl]
    edge = jnp.logical_or(zl == 0, zl == 3)

    def m2(yy, first, second):
        term = jnp.dot(tokg[span((yy % 4) * TOK, TOK), :], wt[...], preferred_element_type=F32)
        first[0:128, :] = term[0:128].astype(first.dtype)
        second[128:256, :] = term[128:256].astype(second.dtype)

    A, B = pl.ds(0, 128), pl.ds(128, 128)

    def p_minus(i):
        slot, rows = ((0, A), (1, B), (1, A))[i]
        dst = (fwd, direct, chain)[i]
        return rcopy(pvs.at[slot, rows], dst.at[rows], ops.at[0, i], opr.at[0, i], at_y(3))

    def p_plus(i):
        slot, rows = ((0, B), (2, A), (2, B))[i]
        dst = (fwd, direct, chain)[i]
        return rcopy(pvs.at[slot, rows], dst.at[rows], ops.at[1, i], opr.at[1, i], at_y(1))

    def opposite():
        m2(y + 2, pvs.at[0], pvs.at[0])
        p_minus(0).start()
        p_plus(0).start()

    def ends(i, h):
        @pl.when(edge)
        def _():
            combine(order[i], h)

    def middle(i, h):
        @pl.when(jnp.logical_not(edge))
        def _():
            combine(order[i], h)

    y_wait(0, 1)
    y_wait(0, 2)
    tok_in.wait()
    tok_wait(0)
    turn(order[0])
    m1(order[0], 0)
    turn(order[1])
    m1(order[1], 0)
    ends(0, 0)
    s3[me_t] = reduced(s2, s2_copy, 4)
    for d in range(1, 8):
        s3_copy(d).start()
    ends(1, 0)
    y_pass(1)
    y_start(2)
    at_distance(2, z_pass)
    tok_wait(1)
    turn(order[2])
    m1(order[2], 0)
    turn(order[3])
    m1(order[3], 0)
    ends(2, 0)
    middle(0, 0)
    y_wait(1, 1)
    y_wait(1, 2)
    m1(order[0], 1)
    m1(order[1], 1)
    ends(0, 1)
    middle(1, 0)
    m1(order[2], 1)
    ends(1, 1)
    y_pass(2)
    m1(order[3], 1)
    ends(2, 1)

    tot = reduced(s3, s3_copy, 8)
    total = jnp.sum(jnp.sum(tot, axis=0, keepdims=True), axis=1, keepdims=True)
    scale = total / (D * FF) + EPSILON
    bound = 0.5 * scale
    plus = scale.astype(BF16).astype(F32)

    def tern(b, from_left=None):
        c_recv(b).wait_recv()

        @pl.loop(0, 16)
        def _(i):
            wide = wg[b, i // 8, span((i % 8) * 16, 16), :].astype(F32)
            value = jnp.where(wide > bound, plus, jnp.where(wide < -bound, -plus, 0.0))
            wt[span(b * 256 + i * 16, 16), :] = value.astype(BF16)

    def m3(yy, half):
        yy = yy % 4
        for j in range(2):
            tt_send[half, yy, :, j * 256:(j + 1) * 256] = lax.dot_general(
                ucg[span(yy * TOK, TOK), :], wt[span(j * 512 + half * 256, 256), :],
                (((1,), (1,)), ((), ())), preferred_element_type=F32,
            ).astype(BF16)
        for d in (2, 1, 3):
            t_send(yy, d, half).start()

    def t_send(yy, d, half):
        return rcopy(
            tt_send.at[half, yy, span(((x + d) % 4) * 64, 64)], tt_recv.at[half, yy, d - 1],
            tts.at[half, yy, d - 1], ttr.at[half, yy, d - 1], at_x(d),
        )

    early, late = zl // 2, 1 - zl // 2

    tern(zl)
    at_distance(1, tern)
    at_distance(2, tern)
    at_distance(3, z_pass)
    middle(2, 0)
    m3(y, early)
    y_wait(2, 1)
    m3(y + 1, early)
    m3(y + 3, early)
    at_distance(3, tern)
    opposite()
    middle(0, 1)
    y_wait(2, 2)
    m3(y + 2, early)
    m1(order[0], 2)
    m1(order[1], 2)
    ends(0, 2)
    m2(y + 3, pvf.at[1], pvs.at[1])
    p_minus(1).start()
    m2(y + 1, pvs.at[2], pvf.at[1])
    p_plus(1).start()
    middle(1, 1)
    m3(y, late)
    m3(y + 1, late)
    ends(1, 2)
    m1(order[2], 2)
    m3(y + 3, late)
    m3(y + 2, late)
    ends(2, 2)
    middle(2, 1)
    m1(order[3], 2)

    def z_copy(half):
        return rcopy(tgr.at[half, 1 - zh], zrecv.at[half], zxs.at[half], zxr.at[half], flip)

    def f_send(yy, j, half):
        return rcopy(
            fsend.at[half, yy, j], tgr.at[half, y // 2, span(x * 64, 64)],
            fs.at[half, yy, j], fr.at[half, y // 2, x], final_dev(yy, j),
        )

    def f_recv(z, xx, half):
        return rcopy(
            fsend.at[half, 0, 0], tgr.at[half, z, span(xx * 64, 64)],
            fs.at[half, 0, 0], fr.at[half, z, xx], final_dev(0, 0),
        )

    def sum_x(half):
        for i in (0, 1, 3, 2):
            yy = (y + i) % 4
            for d in range(1, 4):
                t_send(yy, d, half).wait_recv()

            @pl.loop(0, 4)
            def _(r):
                rows = span(r * 16, 16)
                total = tt_send[half, yy, span(x * 64 + r * 16, 16), :].astype(F32)
                for d in range(1, 4):
                    total = total + tt_recv[half, yy, d - 1, rows, :].astype(F32)
                fsend[half, yy, 0, rows, :] = total[:, 0:256].astype(BF16)
                fsend[half, yy, 1, rows, :] = total[:, 256:512].astype(BF16)

            for j in range(2):
                @pl.when(jnp.logical_not(final_self(yy, j)))
                def _():
                    f_send(yy, j, half).start()

                @pl.when(final_self(yy, j))
                def _():
                    tgr[half, y // 2, span(x * 64, 64), :] = fsend[half, yy, j]

    def to_z(half):
        for z in range(2):
            for xx in range(4):
                @pl.when(jnp.logical_not(source_self(z, xx)))
                def _():
                    f_recv(z, xx, half).wait_recv()

        z_copy(half).start()

    def add_fwd(slot, h):
        @pl.loop(h * 8, h * 8 + 8)
        def _(i):
            rows = span(i * 16, 16)
            pvs[slot, rows, :] = (pvf[1, rows, :] + fwd[rows, :].astype(F32)).astype(BF16)

    sum_x(early)
    middle(0, 2)
    m2(y, pvf.at[0], pvf.at[0])
    middle(1, 2)
    p_minus(0).wait_recv()
    add_fwd(1, 0)
    p_plus(0).wait_recv()
    add_fwd(2, 1)
    middle(2, 2)
    sum_x(late)
    p_minus(2).start()
    p_plus(2).start()
    to_z(early)

    for d in range(1, 4):
        tok_send(d).wait_send()
        s2_copy(d).wait_send()
        for b in range(4):
            t_send(b, d, 0).wait_send()
            t_send(b, d, 1).wait_send()
        for e in range(1, 4):
            tok_share(d, e, 0).wait_send()
            tok_share(d, e, 1).wait_send()
    for d in range(1, 8):
        s1_copy(d).wait_send()
        s3_copy(d).wait_send()
    for i in range(3):
        for h in range(3):
            y_right(h, i).wait_send()
            y_left(h, i).wait_send()
    for b in range(4):
        c_send(b).wait_send()
        for h in range(3):
            g_cross(b, h).wait_send()

        @pl.when(jnp.logical_and(zl < 3, b <= zl))
        def _():
            z_right(b).wait_send()

        @pl.when(jnp.logical_and(zl > 0, b >= zl))
        def _():
            z_left(b).wait_send()

    to_z(late)

    def finish(h):
        @pl.loop(h * 8, h * 8 + 8)
        def _(i):
            rows = span(i * 16, 16)
            up = pvf[0, rows, :] + chain[rows, :].astype(F32) + direct[rows, :].astype(F32)
            hidden_out[rows, :] = (fa[rows, :] * up).astype(BF16)
            gate_out[rows, :] = (fb[rows, :] * up).astype(BF16)

    p_plus(1).wait_recv()
    p_minus(2).wait_recv()
    finish(0)
    p_minus(1).wait_recv()
    p_plus(2).wait_recv()
    finish(1)

    for h in range(3):
        g_cross(zl, h).wait_recv()
        up_out[:, cols(h)] = gp[zl, :, cols(h)] + gxr[zl, :, cols(h)].astype(F32)

        @pl.when(zl > 0)
        def _():
            g_right(zl, h).wait_recv()
            up_out[:, cols(h)] += grl[zl, :, cols(h)].astype(F32)

        @pl.when(zl < 3)
        def _():
            g_left(zl, h).wait_recv()
            up_out[:, cols(h)] += grr[zl, :, cols(h)].astype(F32)

    for half in (early, late):
        z_copy(half).wait_recv()
        token_out[:, span(half * 256, 256)] = (
            tgr[half, zh].astype(F32) + zrecv[half].astype(F32)
        ).astype(BF16)

    for i in range(3):
        p_minus(i).wait_send()
        p_plus(i).wait_send()
    for b in range(4):
        for h in range(3):
            @pl.when(b > zl)
            def _():
                g_right(b, h).wait_send()

            @pl.when(b < zl)
            def _():
                g_left(b, h).wait_send()

    for half in range(2):
        z_copy(half).wait_send()
        for yy in range(4):
            for j in range(2):
                @pl.when(jnp.logical_not(final_self(yy, j)))
                def _():
                    f_send(yy, j, half).wait_send()


def on_device(tokens, gate_values, up_latent, hidden_grad):
    dma = pltpu.SemaphoreType.DMA
    vm = pltpu.VMEM
    return pl.pallas_call(
        kernel,
        out_shape=(
            vm((TOK, COLS), BF16),
            vm((TOK, COLS), BF16),
            vm((TOK, 512), BF16),
            vm((ROWS, COLS), F32),
        ),
        in_specs=[pl.BlockSpec(memory_space=pl.ANY)] * 4,
        out_specs=(pl.BlockSpec(memory_space=pltpu.VMEM),) * 4,
        scratch_shapes=[
            vm((ROWS, COLS), F32),
            vm((4, 2, ROWS, COLS), BF16),
            vm((BLOCK, COLS), BF16),
            vm((BLOCK, BLOCK), BF16),
            vm((4, 256, BLOCK), BF16),
            vm((BLOCK, COLS), BF16),
            vm((TOK, COLS), BF16),
            vm((TOK, COLS), BF16),
            vm((TOK, COLS), F32),
            vm((TOK, COLS), F32),
            vm((4, ROWS, COLS), F32),
            vm((4, ROWS, COLS), BF16),
            vm((4, ROWS, COLS), BF16),
            vm((4, ROWS, COLS), BF16),
            vm((4, ROWS, COLS), BF16),
            vm((4, ROWS, COLS), BF16),
            vm((2, TOK, COLS), F32),
            vm((3, TOK, COLS), BF16),
            vm((TOK, COLS), BF16),
            vm((TOK, COLS), BF16),
            vm((TOK, COLS), BF16),
            vm((2, 4, TOK, 512), BF16),
            vm((2, 4, 3, 64, 512), BF16),
            vm((2, TOK, 256), BF16),
            vm((2, 4, 2, 64, 256), BF16),
            vm((2, 2, TOK, 256), BF16),
            vm((8, 8, 128), F32),
            vm((4, 8, 128), F32),
            vm((8, 8, 128), F32),
            dma((4,)),
            dma((4,)), dma((4,)), dma((4,)), dma((4,)), dma((4,)),
            dma((3, 3)), dma((3, 3)), dma((3, 3)), dma((3, 3)), dma((4,)), dma((4,)), dma((3, 3, 2)), dma((3, 3, 2)),
            dma((8,)), dma((8,)), dma((4,)), dma((4,)), dma((8,)), dma((8,)),
            dma((4, 3)), dma((4, 3)), dma((4, 3)), dma((4, 3)), dma((4, 3)), dma((4, 3)),
            dma((2, 3)), dma((2, 3)), dma((2, 4, 3)), dma((2, 4, 3)), dma((2,)), dma((2,)), dma((2, 4, 2)), dma((2, 2, 4)),
        ],
        compiler_params=pltpu.CompilerParams(
            collective_id=0, has_side_effects=True, vmem_limit_bytes=60 * 1024 * 1024
        ),
    )(tokens, gate_values, up_latent, hidden_grad)


def solution(mesh):
    placed = (P("dp", None), P("dp", "tensor"), P("dp", "tensor"), P("dp", "tensor"))
    return jax.shard_map(
        on_device,
        mesh=mesh,
        in_specs=placed,
        out_specs=(P("dp", "tensor"), P("dp", "tensor"), P("dp", "tensor"), P("dp", "tensor")),
        check_vma=False,
    )
```

```python
import functools

import jax
import jax.numpy as jnp
from jax import lax
from jax.experimental import pallas as pl
from jax.experimental.pallas import tpu as pltpu
from jax.sharding import PartitionSpec as P

D = 4096
FF = 14336
TOK = 256
COLS = 1792
PARTS = ((0, 512), (512, 640), (1152, 640))
ROWS = 128
BLOCK = 1024
EPSILON = 1e-05
MESH = pl.DeviceIdType.MESH
F32 = jnp.float32
BF16 = jnp.bfloat16


def kernel(
    tokens, gate, latent, cot,
    hidden_out, gate_out, token_out, up_out,
    lat32, wg, wt, tokg, tokt, ucg, gate_v, cot_v, fa, fb,
    gp, gxs, gxr, gsend, grl, grr,
    pvf, pvs, fwd, chain, direct,
    tt_send, tt_recv, zrecv, fsend, tgr,
    s1, s2, s3,
    in_sem, zr_sem, zsr_sem, zsl_sem, cs_sem, cr_sem,
    yrs, yrr, yls, ylr, tks, tkr, txs, txr,
    s1s, s1r, s2s, s2r, s3s, s3r,
    gcs, gcr, glr, grs, grr_sem,
    ops, opr, tts, ttr, zxs, zxr, fs, fr,
):
    me_dp = lax.axis_index("dp")
    me_t = lax.axis_index("tensor")
    y = me_dp // 8
    g8 = me_dp % 8
    zl = g8 // 2
    k = g8 % 2
    x = me_t % 4
    zh = me_t // 4

    def dp_of(yy, zz, kk):
        return yy * 8 + zz * 2 + kk

    def at_y(d):
        return (((y + d) % 4) * 8 + g8, me_t)

    def at_z(zz):
        return (dp_of(y, zz, k), me_t)

    other = (dp_of(y, zl, 1 - k), me_t)

    def at_x(d):
        return (me_dp, zh * 4 + (x + d) % 4)

    flip = (me_dp, (1 - zh) * 4 + x)

    def rcopy(src, dst, ssem, rsem, dev):
        return pltpu.make_async_remote_copy(
            src_ref=src, dst_ref=dst, send_sem=ssem, recv_sem=rsem,
            device_id=dev, device_id_type=MESH,
        )

    def final_dev(yy, j):
        return (dp_of(yy, zl, k), zh * 4 + 2 * (y % 2) + j)

    def final_self(yy, j):
        return jnp.logical_and(yy == y, 2 * (y % 2) + j == x)

    def source_self(z, xx):
        return jnp.logical_and(x // 2 + 2 * z == y, xx == x)

    def span(start, size):
        return pl.ds(pl.multiple_of(start, size), size)

    lat_in = pltpu.make_async_copy(latent, lat32, in_sem.at[0])
    gate_in = pltpu.make_async_copy(gate, gate_v, in_sem.at[1])
    cot_in = pltpu.make_async_copy(cot, cot_v, in_sem.at[2])
    tok_in = pltpu.make_async_copy(
        tokens.at[:, span(y * BLOCK, BLOCK)], tokg.at[span(y * TOK, TOK)], in_sem.at[3]
    )
    lat_in.start()
    gate_in.start()
    cot_in.start()
    tok_in.start()

    barrier = pltpu.get_barrier_semaphore()

    def greet(dev):
        pl.semaphore_signal(barrier, inc=1, device_id=dev, device_id_type=MESH)

    for d in range(1, 4):
        greet(at_y(d))
    for d in range(1, 8):
        greet((y * 8 + (g8 + d) % 8, me_t))
    for d in range(1, 4):
        greet(at_x(d))
    for d in range(8):
        greet((y * 8 + d, (1 - zh) * 4 + x))

    for z in range(2):
        for xx in range(4):
            @pl.when(jnp.logical_not(source_self(z, xx)))
            def _():
                greet((dp_of(x // 2 + 2 * z, zl, k), zh * 4 + xx))

    takers = jnp.int32(8)
    for yy in range(4):
        for j in range(2):
            takers = takers - jnp.where(final_self(yy, j), 1, 0)
    pl.semaphore_wait(barrier, 21 + takers)

    def tok_send(d):
        yy = (y + d) % 4
        return rcopy(
            tokens.at[span(x * 64, 64), span(yy * BLOCK, BLOCK)],
            tokg.at[span(y * TOK + x * 64, 64)],
            tks.at[d], tkr.at[d], at_y(d),
        )

    def tok_share(d, e, c):
        half = zl // 2 if c else 1 - zl // 2
        piece = tokg.at[span(((y + 4 - d) % 4) * TOK + x * 64, 64), span(half * 512, 512)]
        return rcopy(piece, piece, txs.at[c], txr.at[c], at_x(e))

    for d in (1, 3, 2):
        tok_send(d).start()

    lat_in.wait()

    def cast_rows(i, acc):
        rows = span(i * 16, 16)
        half = lat32[rows, :].astype(BF16)
        wg[zl, k, rows, :] = half
        mag = jnp.abs(half.astype(F32))
        mag = mag[0:8] + mag[8:16]
        tot = mag[:, 0:128]
        for c in range(1, COLS // 128):
            tot = tot + mag[:, c * 128:(c + 1) * 128]
        return acc + tot

    part = lax.fori_loop(0, ROWS // 16, cast_rows, jnp.zeros((8, 128), F32))

    def z_right(b):
        return rcopy(wg.at[b, k], wg.at[b, k], zsr_sem.at[b], zr_sem.at[b], at_z(lax.rem(zl + 1, 4)))

    def z_left(b):
        return rcopy(wg.at[b, k], wg.at[b, k], zsl_sem.at[b], zr_sem.at[b], at_z(lax.rem(zl + 3, 4)))

    def c_send(b):
        return rcopy(wg.at[b, k], wg.at[b, k], cs_sem.at[b], cr_sem.at[b], other)

    def c_recv(b):
        return rcopy(wg.at[b, k], wg.at[b, 1 - k], cs_sem.at[b], cr_sem.at[b], other)

    me16 = zh * 8 + g8
    s1[me16] = part

    def s1_copy(d):
        to = (me16 + d) % 16
        return rcopy(s1.at[me16], s1.at[me16], s1s, s1r, (y * 8 + to % 8, (to // 8) * 4 + x))

    def s2_copy(d):
        return rcopy(s2.at[y], s2.at[y], s2s, s2r, at_y(d))

    def s3_copy(d):
        return rcopy(s3.at[x], s3.at[x], s3s, s3r, at_x(d))

    for d in range(1, 16):
        s1_copy(d).start()

    @pl.when(zl < 3)
    def _():
        z_right(zl).start()

    @pl.when(zl > 0)
    def _():
        z_left(zl).start()

    c_send(zl).start()


    gate_in.wait()
    cot_in.wait()

    def cot_rows(lo, hi):
        @pl.loop(lo // 16, hi // 16)
        def _(i):
            rows = span(i * 16, 16)
            g = gate_v[rows, :].astype(F32)
            act = g * jax.nn.sigmoid(g)
            ucg[span(y * TOK + i * 16, 16), :] = (cot_v[rows, :].astype(F32) * act).astype(BF16)

    def cols(h):
        return pl.ds(*PARTS[h])

    def uc_part(yy, rows, h):
        return ucg.at[span((yy % 4) * TOK + rows * 128, 128), cols(h)]

    def y_right(h, i):
        piece = (uc_part(y, 0, h), uc_part(y, 1, h), uc_part(y + 3, 0, h))[i]
        return rcopy(piece, piece, yrs, yrr.at[h, i], at_y(1))

    def y_left(h, i):
        piece = (uc_part(y, 1, h), uc_part(y, 0, h), uc_part(y + 1, 1, h))[i]
        return rcopy(piece, piece, yls, ylr.at[h, i], at_y(3))

    def y_start(h):
        y_right(h, 0).start()
        y_left(h, 0).start()
        y_right(h, 1).start()
        y_left(h, 1).start()

    def y_pass(h):
        y_right(h, 0).wait_recv()
        y_right(h, 2).start()
        y_left(h, 0).wait_recv()
        y_left(h, 2).start()

    def y_wait(h, i):
        y_right(h, i).wait_recv()
        y_left(h, i).wait_recv()

    cot_rows(0, 256)
    y_start(0)

    def others(slots, ssem, rsem, n):
        part = slots.at[pl.ds(0, n - 1)]
        return rcopy(part, part, ssem, rsem, other)

    def reduced(slots, ssem, rsem, n):
        others(slots, ssem, rsem, n).wait_recv()
        tot = slots[0]
        for i in range(1, n):
            tot = tot + slots[i]
        return tot

    s2[y] = reduced(s1, s1s, s1r, 16)
    for d in range(1, 4):
        s2_copy(d).start()

    @pl.loop(0, TOK // 16)
    def _(i):
        rows = span(i * 16, 16)
        g = gate_v[rows, :].astype(F32)
        sig = jax.nn.sigmoid(g)
        fa[rows, :] = g * sig
        fb[rows, :] = cot_v[rows, :].astype(F32) * sig * (1.0 + g * (1.0 - sig))

    for d in (1, 3, 2):
        tok_send(d).wait_recv()
        for e in (2, 1, 3):
            tok_share(d, e, 0).start()
    for d in (1, 3, 2):
        for e in (2, 1, 3):
            tok_share(d, e, 1).start()

    def at_distance(s, do):
        @pl.when(zl - s >= 0)
        def _():
            do(lax.rem(zl - s + 4, 4), True)

        @pl.when(zl + s <= 3)
        def _():
            do(lax.rem(zl + s, 4), False)

    def z_pass(b, from_left):
        if from_left:
            z_right(b).wait_recv()

            @pl.when(zl < 3)
            def _():
                z_right(b).start()
        else:
            z_left(b).wait_recv()

            @pl.when(zl > 0)
            def _():
                z_left(b).start()

        c_send(b).start()

    at_distance(1, z_pass)
    y_pass(0)
    y_start(1)
    def turn(target):
        tokt[target, 0:128, :] = tokg[:, span(target * 256 + k * 128, 128)].T
        tokt[target, 128:256, :] = tokg[:, span(target * 256 + (1 - k) * 128, 128)].T

    def tok_all(c):
        part = tokg.at[pl.ds(0, 576), pl.ds(0, 512)]
        return rcopy(part, part, txs.at[c], txr.at[c], at_x(1))

    def tok_wait(c):
        tok_all(c).wait_recv()

    def z_copy(half):
        return rcopy(tgr.at[half, 1 - zh], zrecv.at[half], zxs.at[half], zxr.at[half], flip)

    def f_send(yy, j, half):
        return rcopy(
            fsend.at[half, yy, j], tgr.at[half, y // 2, span(x * 64, 64)],
            fs.at[half, yy, j], fr.at[half, y // 2, x], final_dev(yy, j),
        )

    def f_recv(z, xx, half):
        return rcopy(
            fsend.at[half, 0, 0], tgr.at[half, z, span(xx * 64, 64)],
            fs.at[half, 0, 0], fr.at[half, z, xx], final_dev(0, 0),
        )

    def t_all(half):
        return rcopy(tt_recv.at[half], tt_recv.at[half], tts.at[half], ttr.at[half], at_x(1))

    def sum_x(half):
        t_all(half).wait_recv()
        for i in (0, 1, 3, 2):
            yy = (y + i) % 4

            @pl.loop(0, 4)
            def _(r):
                rows = span(r * 16, 16)
                total = tt_send[half, yy, span(x * 64 + r * 16, 16), :].astype(F32)
                for d in range(1, 4):
                    total = total + tt_recv[half, yy, d - 1, rows, :].astype(F32)
                fsend[half, yy, 0, rows, :] = total[:, 0:256].astype(BF16)
                fsend[half, yy, 1, rows, :] = total[:, 256:512].astype(BF16)

            for j in range(2):
                @pl.when(jnp.logical_not(final_self(yy, j)))
                def _():
                    f_send(yy, j, half).start()

                @pl.when(final_self(yy, j))
                def _():
                    tgr[half, y // 2, span(x * 64, 64), :] = fsend[half, yy, j]

    def to_z(half):
        for z in range(2):
            for xx in range(4):
                @pl.when(jnp.logical_not(source_self(z, xx)))
                def _():
                    f_recv(z, xx, half).wait_recv()

        z_copy(half).start()

    def m1(target, h):
        term = jnp.dot(tokt[target], ucg[:, cols(h)], preferred_element_type=F32)
        gp[target, :, cols(h)] = term[0:128]
        gxs[target, :, cols(h)] = term[128:256].astype(BF16)
        g_cross(target, h).start()

    def part_of(ref, target, h):
        return ref.at[target, :, cols(h)]

    def g_cross(target, h):
        return rcopy(part_of(gxs, target, h), part_of(gxr, target, h), gcs, gcr.at[target, h], other)

    def g_right(target, h):
        return rcopy(
            part_of(gsend, target, h), part_of(grl, target, h),
            grs.at[target, h], glr.at[target, h], at_z(lax.rem(zl + 1, 4)),
        )

    def g_left(target, h):
        return rcopy(
            part_of(gsend, target, h), part_of(grr, target, h),
            grs.at[target, h], grr_sem.at[target, h], at_z(lax.rem(zl + 3, 4)),
        )

    def add_up(target, h, extra):
        @pl.loop(0, ROWS // 16)
        def _(i):
            rows = span(i * 16, 16)
            value = gp[target, rows, cols(h)] + gxr[target, rows, cols(h)].astype(F32)
            if extra is not None:
                value = value + extra[target, rows, cols(h)].astype(F32)
            gsend[target, rows, cols(h)] = value.astype(BF16)

    def combine(target, h):
        g_cross(target, h).wait_recv()

        @pl.when(target > zl)
        def _():
            @pl.when(zl == 0)
            def _():
                add_up(target, h, None)

            @pl.when(zl > 0)
            def _():
                g_right(target, h).wait_recv()
                add_up(target, h, grl)

            g_right(target, h).start()

        @pl.when(target < zl)
        def _():
            @pl.when(zl == 3)
            def _():
                add_up(target, h, None)

            @pl.when(zl < 3)
            def _():
                g_left(target, h).wait_recv()
                add_up(target, h, grr)

            g_left(target, h).start()

    def pick(a0, a1, a2, a3):
        return jnp.where(zl == 0, a0, jnp.where(zl == 1, a1, jnp.where(zl == 2, a2, a3)))

    order = [pick(3, 3, 0, 0), pick(2, 2, 1, 1), pick(1, 0, 3, 2), zl]
    edge = jnp.logical_or(zl == 0, zl == 3)

    def m2(yy, first, second):
        term = jnp.dot(tokg[span((yy % 4) * TOK, TOK), :], wt[...], preferred_element_type=F32)
        first[0:128, :] = term[0:128].astype(first.dtype)
        second[128:256, :] = term[128:256].astype(second.dtype)

    A, B = pl.ds(0, 128), pl.ds(128, 128)

    def p_minus(i):
        slot, rows = ((0, A), (1, B), (1, A))[i]
        dst = (fwd, direct, chain)[i]
        return rcopy(pvs.at[slot, rows], dst.at[rows], ops.at[0, i], opr.at[0, i], at_y(3))

    def p_plus(i):
        slot, rows = ((0, B), (2, A), (2, B))[i]
        dst = (fwd, direct, chain)[i]
        return rcopy(pvs.at[slot, rows], dst.at[rows], ops.at[1, i], opr.at[1, i], at_y(1))

    def opposite():
        m2(y + 2, pvs.at[0], pvs.at[0])
        p_minus(0).start()
        p_plus(0).start()

    def ends(i, h):
        @pl.when(edge)
        def _():
            combine(order[i], h)

    def middle(i, h):
        @pl.when(jnp.logical_not(edge))
        def _():
            combine(order[i], h)

    y_wait(0, 1)
    y_wait(0, 2)
    tok_in.wait()
    tok_wait(0)
    turn(order[0])
    m1(order[0], 0)
    turn(order[1])
    m1(order[1], 0)
    ends(0, 0)
    s3[x] = reduced(s2, s2s, s2r, 4)
    for d in range(1, 4):
        s3_copy(d).start()
    ends(1, 0)
    y_pass(1)
    y_start(2)
    at_distance(2, z_pass)
    tok_wait(1)
    turn(order[2])
    m1(order[2], 0)
    turn(order[3])
    m1(order[3], 0)
    ends(2, 0)
    middle(0, 0)
    tot = reduced(s3, s3s, s3r, 4)
    total = jnp.sum(jnp.sum(tot, axis=0, keepdims=True), axis=1, keepdims=True)
    scale = total / (D * FF) + EPSILON
    bound = 0.5 * scale
    plus = scale.astype(BF16).astype(F32)

    def tern(b, from_left=None):
        c_recv(b).wait_recv()

        @pl.loop(0, 16)
        def _(i):
            wide = wg[b, i // 8, span((i % 8) * 16, 16), :].astype(F32)
            value = jnp.where(wide > bound, plus, jnp.where(wide < -bound, -plus, 0.0))
            wt[span(b * 256 + i * 16, 16), :] = value.astype(BF16)

    def m3(yy, half):
        yy = yy % 4
        for j in range(2):
            tt_send[half, yy, :, j * 256:(j + 1) * 256] = lax.dot_general(
                ucg[span(yy * TOK, TOK), :], wt[span(j * 512 + half * 256, 256), :],
                (((1,), (1,)), ((), ())), preferred_element_type=F32,
            ).astype(BF16)
        for d in (2, 1, 3):
            t_send(yy, d, half).start()

    def t_send(yy, d, half):
        return rcopy(
            tt_send.at[half, yy, span(((x + d) % 4) * 64, 64)], tt_recv.at[half, yy, d - 1],
            tts.at[half], ttr.at[half], at_x(d),
        )

    early, late = zl // 2, 1 - zl // 2

    tern(zl)
    at_distance(1, tern)
    y_wait(1, 1)
    y_wait(1, 2)
    m1(order[0], 1)
    m1(order[1], 1)
    ends(0, 1)
    middle(1, 0)
    m1(order[2], 1)
    ends(1, 1)
    at_distance(2, tern)
    m3(y, early)
    y_pass(2)
    m1(order[3], 1)
    ends(2, 1)

    at_distance(3, z_pass)
    middle(2, 0)
    y_wait(2, 1)
    m3(y + 1, early)
    m3(y + 3, early)
    at_distance(3, tern)
    opposite()
    middle(0, 1)
    y_wait(2, 2)
    m3(y + 2, early)
    m1(order[0], 2)
    m1(order[1], 2)
    ends(0, 2)
    m3(y, late)
    m3(y + 1, late)
    m3(y + 3, late)
    m3(y + 2, late)
    m2(y + 3, pvf.at[1], pvs.at[1])
    m2(y + 1, pvs.at[2], pvf.at[1])
    sum_x(early)
    p_minus(1).start()
    p_plus(1).start()
    ends(1, 2)
    middle(1, 1)
    m1(order[2], 2)
    ends(2, 2)
    middle(2, 1)
    m1(order[3], 2)

    def add_fwd(slot, h):
        @pl.loop(h * 8, h * 8 + 8)
        def _(i):
            rows = span(i * 16, 16)
            pvs[slot, rows, :] = (pvf[1, rows, :] + fwd[rows, :].astype(F32)).astype(BF16)

    middle(0, 2)
    m2(y, pvf.at[0], pvf.at[0])
    middle(1, 2)
    p_minus(0).wait_recv()
    add_fwd(1, 0)
    p_plus(0).wait_recv()
    add_fwd(2, 1)
    middle(2, 2)
    to_z(early)
    sum_x(late)
    p_minus(2).start()
    p_plus(2).start()

    t_all(0).wait_send()
    t_all(1).wait_send()
    tok_all(0).wait_send()
    tok_all(1).wait_send()
    for d in range(1, 4):
        tok_send(d).wait_send()
    others(s1, s1s, s1r, 16).wait_send()
    others(s2, s2s, s2r, 4).wait_send()
    others(s3, s3s, s3r, 4).wait_send()
    rcopy(gxs, gxr, gcs, gcr.at[0, 0], other).wait_send()
    all_sent = ucg.at[pl.ds(0, 384)]
    rcopy(all_sent, all_sent, yrs, yrr.at[0, 0], at_y(1)).wait_send()
    rcopy(all_sent, all_sent, yls, ylr.at[0, 0], at_y(3)).wait_send()
    for b in range(4):
        c_send(b).wait_send()
        @pl.when(jnp.logical_and(zl < 3, b <= zl))
        def _():
            z_right(b).wait_send()

        @pl.when(jnp.logical_and(zl > 0, b >= zl))
        def _():
            z_left(b).wait_send()

    to_z(late)

    def finish(h):
        @pl.loop(h * 8, h * 8 + 8)
        def _(i):
            rows = span(i * 16, 16)
            up = pvf[0, rows, :] + chain[rows, :].astype(F32) + direct[rows, :].astype(F32)
            hidden_out[rows, :] = (fa[rows, :] * up).astype(BF16)
            gate_out[rows, :] = (fb[rows, :] * up).astype(BF16)

    p_plus(1).wait_recv()
    p_minus(2).wait_recv()
    finish(0)
    p_minus(1).wait_recv()
    p_plus(2).wait_recv()
    finish(1)

    for h in range(3):
        g_cross(zl, h).wait_recv()
        up_out[:, cols(h)] = gp[zl, :, cols(h)] + gxr[zl, :, cols(h)].astype(F32)

        @pl.when(zl > 0)
        def _():
            g_right(zl, h).wait_recv()
            up_out[:, cols(h)] += grl[zl, :, cols(h)].astype(F32)

        @pl.when(zl < 3)
        def _():
            g_left(zl, h).wait_recv()
            up_out[:, cols(h)] += grr[zl, :, cols(h)].astype(F32)

    for half in (early, late):
        z_copy(half).wait_recv()
        token_out[:, span(half * 256, 256)] = (
            tgr[half, zh].astype(F32) + zrecv[half].astype(F32)
        ).astype(BF16)

    for i in range(3):
        p_minus(i).wait_send()
        p_plus(i).wait_send()
    for b in range(4):
        for h in range(3):
            @pl.when(b > zl)
            def _():
                g_right(b, h).wait_send()

            @pl.when(b < zl)
            def _():
                g_left(b, h).wait_send()

    for half in range(2):
        z_copy(half).wait_send()
        for yy in range(4):
            for j in range(2):
                @pl.when(jnp.logical_not(final_self(yy, j)))
                def _():
                    f_send(yy, j, half).wait_send()


def on_device(tokens, gate_values, up_latent, hidden_grad):
    dma = pltpu.SemaphoreType.DMA
    vm = pltpu.VMEM
    return pl.pallas_call(
        kernel,
        out_shape=(
            vm((TOK, COLS), BF16),
            vm((TOK, COLS), BF16),
            vm((TOK, 512), BF16),
            vm((ROWS, COLS), F32),
        ),
        in_specs=[pl.BlockSpec(memory_space=pl.ANY)] * 4,
        out_specs=(pl.BlockSpec(memory_space=pltpu.VMEM),) * 4,
        scratch_shapes=[
            vm((ROWS, COLS), F32),
            vm((4, 2, ROWS, COLS), BF16),
            vm((BLOCK, COLS), BF16),
            vm((BLOCK, BLOCK), BF16),
            vm((4, 256, BLOCK), BF16),
            vm((BLOCK, COLS), BF16),
            vm((TOK, COLS), BF16),
            vm((TOK, COLS), BF16),
            vm((TOK, COLS), F32),
            vm((TOK, COLS), F32),
            vm((4, ROWS, COLS), F32),
            vm((4, ROWS, COLS), BF16),
            vm((4, ROWS, COLS), BF16),
            vm((4, ROWS, COLS), BF16),
            vm((4, ROWS, COLS), BF16),
            vm((4, ROWS, COLS), BF16),
            vm((2, TOK, COLS), F32),
            vm((3, TOK, COLS), BF16),
            vm((TOK, COLS), BF16),
            vm((TOK, COLS), BF16),
            vm((TOK, COLS), BF16),
            vm((2, 4, TOK, 512), BF16),
            vm((2, 4, 3, 64, 512), BF16),
            vm((2, TOK, 256), BF16),
            vm((2, 4, 2, 64, 256), BF16),
            vm((2, 2, TOK, 256), BF16),
            vm((16, 8, 128), F32),
            vm((4, 8, 128), F32),
            vm((4, 8, 128), F32),
            dma((4,)),
            dma((4,)), dma((4,)), dma((4,)), dma((4,)), dma((4,)),
            dma, dma((3, 3)), dma, dma((3, 3)), dma((4,)), dma((4,)), dma((2,)), dma((2,)),
            dma, dma, dma, dma, dma, dma,
            dma, dma((4, 3)), dma((4, 3)), dma((4, 3)), dma((4, 3)),
            dma((2, 3)), dma((2, 3)), dma((2,)), dma((2,)), dma((2,)), dma((2,)), dma((2, 4, 2)), dma((2, 2, 4)),
        ],
        compiler_params=pltpu.CompilerParams(
            collective_id=0, has_side_effects=True, vmem_limit_bytes=60 * 1024 * 1024
        ),
    )(tokens, gate_values, up_latent, hidden_grad)


def solution(mesh):
    placed = (P("dp", None), P("dp", "tensor"), P("dp", "tensor"), P("dp", "tensor"))
    return jax.shard_map(
        on_device,
        mesh=mesh,
        in_specs=placed,
        out_specs=(P("dp", "tensor"), P("dp", "tensor"), P("dp", "tensor"), P("dp", "tensor")),
        check_vma=False,
    )
```
